128 devices in a mesh: row: 8 (over y, core), col: 8 (over x_hi, z), head: 2 (over x_lo).
Axes of the slice: x: 4 (x_hi: 2, x_lo: 2; x = x_hi * 2 + x_lo), y: 4, z: 4, core: 2. Of those that a mesh axis runs over, the one named last changes fastest.
Arguments:
- queries: bfloat16 [6144, 4096], P('row', ('head', 'col')), may hold values from -10 to 10
- key_states: bfloat16 [6144, 4096], P('col', ('head', 'row')), may hold values from -10 to 10
- value_states: bfloat16 [6144, 4096], P('col', ('head', 'row')), may hold values from -6 to 6
- out_grad: bfloat16 [6144, 4096], P('row', ('head', 'col')), may hold values from -6 to 6
Outputs:
- query_grad: bfloat16 [6144, 4096], P('row', ('head', 'col'))
- key_grad: bfloat16 [6144, 4096], P('col', ('head', 'row'))
- value_grad: bfloat16 [6144, 4096], P('col', ('head', 'row'))
The draws below stay inside these ranges and needn't reach their ends.
All inputs are finite; a program needn't handle non-finite values.
Results may differ from the reference program's by a relative error of at most 0.0069.
Values may be sent and summed in bfloat16 or wider, within the bound.
A program may use at most 128 MiB of HBM per device.

```python
import math
import jax
import jax.numpy as jnp
from jax import lax

HEADS = 32
HEAD_DIM = 128
WIDTH = 4096
SEQ = 6144


def draw_queries(key, part):
    key = jax.random.fold_in(key, 3)
    base = jax.random.truncated_normal(key, -4.0, 4.0, (SEQ, HEADS * HEAD_DIM), jnp.float32)
    return base.astype(jnp.bfloat16)


def draw_key_states(key, part):
    key = jax.random.fold_in(key, 4)
    base = jax.random.truncated_normal(key, -4.0, 4.0, (SEQ, HEADS * HEAD_DIM), jnp.float32)
    return base.astype(jnp.bfloat16)


def level_of(rng, shape, pieces, smallest, high):
    def one(axis_at, blocks):
        heights = jax.random.uniform(jax.random.fold_in(jax.random.fold_in(rng, 6), axis_at), (blocks,), jnp.float32, smallest / len(pieces), high / len(pieces))
        return jnp.repeat(jnp.exp(heights), shape[axis_at] // blocks).reshape((-1,) + (1,) * (len(shape) - axis_at - 1))

    level = one(*pieces[0])
    for cut in pieces[1:]:
        level = level * one(*cut)
    return level


def noise(own_key, extent, scale, limit, shards=(), kind=jnp.bfloat16):
    entries = jax.random.normal(own_key, extent, jnp.float32) * scale
    if len(shards) > 0:
        entries = level_of(own_key, extent, shards, -0.22, 0.18) * entries
    return jnp.clip(entries, min=-limit, max=limit).astype(kind)


def setup_inputs(seed: int = 0) -> dict:
    key_of = jax.random.split(jax.random.key(seed), 5)
    return {
        "queries": draw_queries(jax.random.fold_in(key_of[4], 71), 0),
        "key_states": draw_key_states(jax.random.fold_in(key_of[4], 71), 0),
        "value_states": noise(key_of[2], (SEQ, WIDTH), 1.0, 6.0, ((0, 8), (1, 16))),
        "out_grad": noise(key_of[3], (SEQ, WIDTH), 1.0, 6.0, ((0, 8), (1, 16))),
    }


def reference(queries, key_states, value_states, out_grad):
    scaling = 1.0 / math.sqrt(HEAD_DIM)

    def one_head(head_index):
        start = head_index * HEAD_DIM
        query_h = lax.dynamic_slice_in_dim(queries, start, HEAD_DIM, 1)
        key_h = lax.dynamic_slice_in_dim(key_states, start, HEAD_DIM, 1)
        value_h = lax.dynamic_slice_in_dim(value_states, start, HEAD_DIM, 1)
        grad_h = lax.dynamic_slice_in_dim(out_grad, start, HEAD_DIM, 1)
        scores = scaling * jnp.dot(query_h, key_h.T, preferred_element_type=jnp.float32)
        peak = lax.optimization_barrier(jnp.max(scores, axis=1))
        expo = jnp.exp(scores - peak[:, None])
        total = lax.optimization_barrier(jnp.sum(expo, axis=1))
        prob = jnp.exp(scores - peak[:, None]) / total[:, None]
        dprob = jnp.dot(grad_h, value_h.T, preferred_element_type=jnp.float32)
        delta = lax.optimization_barrier(jnp.sum(prob * dprob, axis=1))
        dscore = (prob * (dprob - delta[:, None]) * scaling).astype(jnp.bfloat16)
        prob_low = prob.astype(jnp.bfloat16)
        value_g = jnp.dot(prob_low.T, grad_h, preferred_element_type=jnp.float32).astype(jnp.bfloat16)
        query_g = jnp.dot(dscore, key_h, preferred_element_type=jnp.float32).astype(jnp.bfloat16)
        key_g = jnp.dot(dscore.T, query_h, preferred_element_type=jnp.float32).astype(jnp.bfloat16)
        return (query_g, key_g, value_g)
    query_g, key_g, value_g = lax.map(one_head, jnp.arange(HEADS, dtype=jnp.int32))

    def flatten(stacked):
        return jnp.transpose(stacked, (1, 0, 2)).reshape(SEQ, HEADS * HEAD_DIM)
    return (flatten(query_g), flatten(key_g), flatten(value_g))
```

```python
import math

import jax
import jax.numpy as jnp
from jax import lax
from jax.experimental import pallas as pl
from jax.experimental.pallas import tpu as pltpu
from jax.sharding import PartitionSpec as P

HEAD_DIM = 128
BLK = 768
NB = 4
TILE = 512
TILES = NB * BLK // TILE
HALF = NB * BLK // 2
AUG = 144
SCALE = 1.0 / math.sqrt(HEAD_DIM)
LOG2E = math.log2(math.e)
MESH = pl.DeviceIdType.MESH
F32 = jnp.float32
BF16 = jnp.bfloat16


def order(d):
    return jnp.where(d == 2, 3, jnp.where(d == 3, 2, d))


def z_of(p, j):
    return lax.rem(p, 4) if j == 0 else 3 - lax.rem(p, 4)


def dot(a, b):
    return jnp.dot(a, b, preferred_element_type=F32)


def dot_nt(a, b):
    return lax.dot_general(a, b, (((1,), (1,)), ((), ())), preferred_element_type=F32)


def kernel(
    q_in, k_in, v_in, g_in,
    dq_rx, dk_rx, dv_rx,
    kb, vb, xr, via, qgb, kt, vt, qt, gt, qft, gft,
    s0, s1, prob, ot, stat_tx, stat_rx, rows, dqt, dk_acc, dv_acc,
    dq_tx, sib_tx, sib_rx, kv_tx,
    k_rs, v_rs, xr_rs, via_rs, qg_rs, st_rs, sib_rs, dq_rs, kv_rs,
    home_ss, xr_ss, self_s, fwd_ss, hop_ss, st_ss, sib_ss, dq_ss, kv_ss,
):
    r, col, g = lax.axis_index("row"), lax.axis_index("col"), lax.axis_index("head")
    y, c = r // 2, lax.rem(r, 2)
    xh, z = col // 4, lax.rem(col, 4)
    low = lax.rem(2 * y, 4)
    first = jnp.logical_and(z >= low, z < low + 2)
    pw = jnp.where(first, 2 * y + z - low, 2 * y + 3 - z - low)
    jw = jnp.where(first, 0, 1)
    aw = lax.rem(pw, 2)
    pk, pq = r, col
    partner = (y, c, 1 - xh, z)
    sibling = (y, 1 - c, xh, z)
    relay = c == aw

    up, down = lax.rem(xh + g, 2), lax.rem(xh + 1 - g, 2)

    def dev(t):
        yy, cc, xx, zz = t[:4]
        return (2 * yy + cc, 4 * xx + zz, g if len(t) == 4 else t[4])

    def is_me(t):
        yy, cc, xx, zz = t
        return jnp.logical_and(2 * yy + cc == r, 4 * xx + zz == col)

    barrier = pltpu.get_barrier_semaphore()
    greeted = [partner, sibling] + [(y, c, xx, zz, 1 - g) for xx in (up, down) for zz in (z, 3 - z)]
    greeted += [(lax.rem(y + d, 4), c, xh, z) for d in (1, 2, 3)]
    greeted += [(y, cc, xh, lax.rem(z + d, 4)) for d in (1, 2, 3) for cc in range(2)]
    greeted += [(lax.rem(y + d, 4), c, pw // 4, lax.rem(pw, 4)) for d in range(4)]
    greeted += [(pq // 2, c, xx, z_of(pq, j)) for j in range(2) for xx in range(2)]
    for t in greeted:
        pl.semaphore_signal(barrier, inc=1, device_id=dev(t), device_id_type=MESH)
    pl.semaphore_wait(barrier, len(greeted))

    def remote(src, dst, t, ssem, rsem):
        return pltpu.make_async_remote_copy(
            src_ref=src, dst_ref=dst, send_sem=ssem, recv_sem=rsem, device_id=dev(t), device_id_type=MESH
        )

    def put(src, dst, t, ssem, rsem):
        me = is_me(t)

        @pl.when(jnp.logical_not(me))
        def _():
            remote(src, dst, t, ssem, rsem).start()

        @pl.when(me)
        def _():
            pltpu.make_async_copy(src, dst, rsem).start()

    def sent(src, dst, t, ssem, rsem):
        @pl.when(jnp.logical_not(is_me(t)))
        def _():
            remote(src, dst, t, ssem, rsem).wait_send()

    def arrived(dst, rsem):
        pltpu.make_async_copy(dst, dst, rsem).wait()

    def cols(j):
        return pl.ds(j * HEAD_DIM, HEAD_DIM)

    def spread(arr, ref):
        slot = pq // 2
        pltpu.make_async_copy(ref.at[:, cols(0)], via.at[arr, slot], via_rs.at[arr, slot]).start()
        out = []
        for n, (j, t) in enumerate(((0, (y, c, up, z, 1 - g)), (1, (y, c, down, z, 1 - g)))):
            out.append(remote(ref.at[:, cols(j)], xr.at[arr, n], t, home_ss.at[arr, n], xr_rs.at[arr, n]))
        t = (y, c, xh, 3 - z)
        out.append(remote(ref.at[:, cols(1)], via.at[arr, slot], t, home_ss.at[arr, 2], via_rs.at[arr, slot]))
        for copy in out:
            copy.start()
        return out

    def cross(arr):
        out = []
        for n, (origin, to) in enumerate(((down, (y, c, up, z, 1 - g)), (up, (y, c, down, 3 - z, 1 - g)))):
            slot = (4 * origin + z) // 2
            arrived(xr.at[arr, n], xr_rs.at[arr, n])
            out.append(remote(xr.at[arr, n], via.at[arr, slot], to, xr_ss.at[arr, n], via_rs.at[arr, slot]))
            out[-1].start()
        return out

    def hop(arr):
        out = []
        for n, d in enumerate((1, 3, 2)):
            to = lax.rem(y + d, 4)
            slot = {3: 1, 1: 2, 2: 3}[d]
            arrived(via.at[arr, to], via_rs.at[arr, to])
            out.append(
                remote(via.at[arr, to], qgb.at[arr, slot - 1], (to, c, xh, z), hop_ss.at[arr, n], qg_rs.at[arr, slot - 1])
            )
            out[-1].start()
        return out

    def home_kv(arr, j):
        ref, buf, sem = ((k_in, kb, k_rs), (v_in, vb, v_rs))[arr]
        zz = z_of(pk, j)
        slot = order(lax.rem(z - zz + 4, 4))
        return (ref.at[:, cols(j)], buf.at[slot], (y, c, xh, zz), self_s.at[arr, j], sem.at[slot])

    def forward_kv(arr, n):
        buf, sem = ((kb, k_rs), (vb, v_rs))[arr]
        return remote(buf.at[n], buf.at[n], sibling, fwd_ss.at[arr, n], sem.at[n])

    def span(at, size=TILE):
        return slice(at * size, (at + 1) * size)

    pending = spread(0, q_in)
    for j in range(2):
        put(*home_kv(0, j))
    pending += cross(0)
    arrived(via.at[0, y], via_rs.at[0, y])
    pending += hop(0)
    for j in range(2):
        put(*home_kv(1, j))
    qt[:, span(0, BLK)] = via[0, y].T

    sbuf = (s0, s1)

    def scores(i, n, mx):
        s = dot(kb[n], qt[:, span(i)])
        sbuf[i % 2][n] = s
        return jnp.maximum(mx, jnp.max(s.reshape(BLK // 8, 8, TILE), axis=0))

    lowest = jnp.full((8, TILE), -jnp.inf, F32)

    def first_scores(n, mx):
        arrived(kb.at[n], k_rs.at[n])

        @pl.when(relay)
        def _():
            forward_kv(0, n).start()

        kt[n] = kb[n].T
        return scores(0, n, mx)

    mx = lax.fori_loop(0, NB, first_scores, lowest)
    pending += spread(1, g_in)

    def fetch_v(n, carry):
        arrived(vb.at[n], v_rs.at[n])

        @pl.when(relay)
        def _():
            forward_kv(1, n).start()

        vt[n, :HEAD_DIM, :] = vb[n].T
        vt[n, HEAD_DIM:, :] = jnp.ones((AUG - HEAD_DIM, BLK), BF16)
        return carry

    lax.fori_loop(0, NB, fetch_v, 0)

    def weigh(i, n, m):
        p = jnp.exp2((sbuf[i % 2][n] - m) * (SCALE * LOG2E)).astype(BF16)
        prob[i, n] = p
        ot[:, span(i)] += dot(vt[n], p)

    def stat_copy(half):
        return remote(stat_tx.at[half], stat_rx.at[half], partner, st_ss.at[half], st_rs.at[half])

    def finish(half):
        for b in (2 * half, 2 * half + 1):
            if b == 0:
                arrived(via.at[1, y], via_rs.at[1, y])
                gt[:, span(0, BLK)] = via[1, y].T
            else:
                arrived(qgb.at[1, b - 1], qg_rs.at[1, b - 1])
                gt[:, span(b, BLK)] = qgb[1, b - 1].T
        here = span(half, HALF)
        stat_tx[half, 1:2] = ot[HEAD_DIM : HEAD_DIM + 1, here]
        stat_tx[half, 2:3] = jnp.sum(gt[:, here].astype(F32) * ot[:HEAD_DIM, here], axis=0, keepdims=True)
        stat_copy(half).start()

    ot[...] = jnp.zeros_like(ot)
    for i in range(TILES):
        m = jnp.max(mx, axis=0, keepdims=True)
        stat_tx[i // 3, 0:1, span(i % 3)] = m
        more = i + 1 < TILES
        if i in (0, 2, 3):
            b = max(i, 1)
            arrived(qgb.at[0, b - 1], qg_rs.at[0, b - 1])
            qt[:, span(b, BLK)] = qgb[0, b - 1].T

        def step(n, mx2):
            if more:
                mx2 = scores(i + 1, n, mx2)
            weigh(i, n, m)
            return mx2

        mx = lax.fori_loop(0, NB, step, lowest)
        if i == 0:
            pending += cross(1)
        if i == 1:
            pending += hop(1)
        if i == TILES - 2:
            finish(0)
    finish(1)

    def combine(half):
        stat_copy(half).wait()
        m0, l0, d0 = stat_tx[half, 0:1], stat_tx[half, 1:2], stat_tx[half, 2:3]
        m1, l1, d1 = stat_rx[half, 0:1], stat_rx[half, 1:2], stat_rx[half, 2:3]
        m = jnp.maximum(m0, m1)
        e0 = jnp.exp2((m0 - m) * (SCALE * LOG2E))
        e1 = jnp.exp2((m1 - m) * (SCALE * LOG2E))
        inv = 1.0 / (l0 * e0 + l1 * e1)
        f = e0 * inv
        here = span(half, HALF)
        rows[0:1, here] = (d0 * e0 + d1 * e1) * inv
        rows[1:2, here] = f * SCALE
        gft[:, here] = (gt[:, here].astype(F32) * f).astype(BF16)
        qft[:, here] = (qt[:, here].astype(F32) * (f * SCALE)).astype(BF16)

    dqt[...] = jnp.zeros_like(dqt)
    dk_acc[...] = jnp.zeros_like(dk_acc)
    dv_acc[...] = jnp.zeros_like(dv_acc)

    def dq_args(i):
        t = (lax.rem(y + order(i), 4), c, pw // 4, lax.rem(pw, 4))
        return (dq_tx.at[i], dq_rx.at[jw, xh], t, dq_ss.at[i], dq_rs.at[jw, xh])

    def sib_copy(n):
        return remote(sib_tx.at[n], sib_rx.at[n], sibling, sib_ss.at[n], sib_rs.at[n])

    def kv_args(n, raw):
        t = (y, aw, xh, lax.rem(z + order(n), 4))
        return [(kv_tx.at[n], raw.at[:, cols(j)], t, kv_ss.at[n], kv_rs.at[c, j]) for j in range(2)]

    def by_core(run):
        @pl.when(c == 0)
        def _():
            run(dk_acc, dv_acc, dk_rx)

        @pl.when(c == 1)
        def _():
            run(dv_acc, dk_acc, dv_rx)

    def by_member(run):
        for j in range(2):

            @pl.when(jw == j)
            def _():
                run(j)

    def trade_kv(n):
        def run(_, other, __):
            sib_tx[n] = other[n].astype(BF16)

        by_core(run)
        sib_copy(n).start()

    def reduce_kv(n):
        arrived(sib_rx.at[n], sib_rs.at[n])

        def run(own, _, raw):
            kv_tx[n] = (own[n] + sib_rx[n].astype(F32)).astype(BF16)
            by_member(lambda j: put(*kv_args(n, raw)[j]))

        by_core(run)

    def backward(i, n):
        here = span(i)
        p = prob[i, n]
        dp = dot(vb[n], gt[:, here])
        ds = (p.astype(F32) * (dp - rows[0:1, here])).astype(BF16)
        dv_acc[n] += dot_nt(p, gft[:, here])
        dk_acc[n] += dot_nt(ds, qft[:, here])
        dqt[:, here] += dot(kt[n], ds)

    def send_dq(b):
        here = span(b, BLK)
        dq_tx[b] = (dqt[:, here] * rows[1:2, here]).T.astype(BF16)
        put(*dq_args(b))

    def loop(lo, hi, body):
        def run(n, carry):
            body(n)
            return carry

        lax.fori_loop(lo, hi, run, 0)

    def first_half(n):
        for i in range(3):
            backward(i, n)

    combine(0)
    loop(0, NB, first_half)
    send_dq(0)
    send_dq(1)
    combine(1)

    def second_half(n):
        for i in range(3, 6):
            backward(i, n)
        trade_kv(n)

    loop(0, 2, second_half)
    reduce_kv(jnp.int32(0))

    def most(n):
        for i in range(3, 5):
            backward(i, n)

    loop(2, 4, most)
    send_dq(2)
    reduce_kv(jnp.int32(1))

    def final(n):
        backward(5, n)
        trade_kv(n)

    loop(2, 4, final)
    reduce_kv(jnp.int32(2))
    send_dq(3)
    reduce_kv(jnp.int32(3))

    for j in range(2):
        for n in range(2):
            arrived(dq_rx.at[j, n], dq_rs.at[j, n])
        for arr, raw in ((0, dk_rx), (1, dv_rx)):
            arrived(raw.at[:, cols(j)], kv_rs.at[arr, j])

    for copy in pending:
        copy.wait_send()
    for arr in range(2):
        for j in range(2):
            sent(*home_kv(arr, j))

    @pl.when(relay)
    def _():
        for arr in range(2):
            for n in range(NB):
                forward_kv(arr, n).wait_send()

    for i in range(NB):
        sent(*dq_args(jnp.int32(i)))
        sent(*kv_args(jnp.int32(i), dk_rx)[0])
        sib_copy(i).wait_send()


def collect(dq_raw, dk_raw, dv_raw, dq_out, dk_out, dv_out):
    for j in range(2):
        total = dq_raw[j, 0].astype(F32) + dq_raw[j, 1].astype(F32)
        dq_out[:, j * HEAD_DIM : (j + 1) * HEAD_DIM] = total.astype(BF16)
    dk_out[...] = dk_raw[...]
    dv_out[...] = dv_raw[...]


def per_device(queries, key_states, value_states, out_grad):
    rows, width = queries.shape
    shape = jax.ShapeDtypeStruct((rows, width), BF16)
    vm = pltpu.VMEM
    dma = pltpu.SemaphoreType.DMA
    tile = (NB, BLK, HEAD_DIM)
    tile_t = (NB, HEAD_DIM, BLK)
    flat_t = (HEAD_DIM, NB * BLK)
    flops = 6 * 2 * (NB * BLK) ** 2 * HEAD_DIM
    raw = pl.pallas_call(
        kernel,
        out_shape=(jax.ShapeDtypeStruct((2, 2, BLK, HEAD_DIM), BF16), shape, shape),
        in_specs=[pl.BlockSpec(memory_space=pl.ANY)] * 4,
        out_specs=tuple([pl.BlockSpec(memory_space=pl.ANY)] * 3),
        scratch_shapes=[
            vm(tile, BF16), vm(tile, BF16), vm((2, 2, BLK, HEAD_DIM), BF16), vm((2,) + tile, BF16), vm((2, NB - 1, BLK, HEAD_DIM), BF16),
            vm(tile_t, BF16), vm((NB, AUG, BLK), BF16), vm(flat_t, BF16), vm(flat_t, BF16), vm(flat_t, BF16), vm(flat_t, BF16),
            vm((NB, BLK, TILE), F32), vm((NB, BLK, TILE), F32), vm((TILES, NB, BLK, TILE), BF16), vm((AUG, NB * BLK), F32),
            vm((2, 8, HALF), F32), vm((2, 8, HALF), F32), vm((8, NB * BLK), F32), vm(flat_t, F32),
            vm(tile, F32), vm(tile, F32),
            vm(tile, BF16), vm(tile, BF16), vm(tile, BF16), vm(tile, BF16),
            dma((NB,)), dma((NB,)), dma((2, 2)), dma((2, NB)), dma((2, NB - 1)), dma((NB,)), dma((NB,)), dma((2, 2)), dma((2, 2)),
            dma((2, 3)), dma((2, 2)), dma((2, 2)), dma((2, NB)), dma((2, 3)), dma((NB,)), dma((NB,)), dma((NB,)), dma((NB,)),
        ],
        compiler_params=pltpu.CompilerParams(
            collective_id=0, has_side_effects=True, vmem_limit_bytes=62 * 1024 * 1024
        ),
        cost_estimate=pl.CostEstimate(flops=flops, bytes_accessed=4 * rows * width * 2, transcendentals=(NB * BLK) ** 2),
    )(queries, key_states, value_states, out_grad)
    part = rows // 3
    whole = pl.BlockSpec((part, width), lambda n: (n, 0))
    return pl.pallas_call(
        collect,
        out_shape=(shape, shape, shape),
        grid=(3,),
        in_specs=[pl.BlockSpec((2, 2, part, HEAD_DIM), lambda n: (0, 0, n, 0))] + [whole] * 2,
        out_specs=(whole,) * 3,
    )(*raw)


def solution(mesh):
    placed = (
        P("row", ("head", "col")),
        P("col", ("head", "row")),
        P("col", ("head", "row")),
        P("row", ("head", "col")),
    )
    return jax.shard_map(
        per_device,
        mesh=mesh,
        in_specs=placed,
        out_specs=(P("row", ("head", "col")), P("col", ("head", "row")), P("col", ("head", "row"))),
        check_vma=False,
    )
```

```python
import math

import jax
import jax.numpy as jnp
from jax import lax
from jax.experimental import pallas as pl
from jax.experimental.pallas import tpu as pltpu
from jax.sharding import PartitionSpec as P

HEAD_DIM = 128
BLK = 768
NB = 4
AUG = 144
SCALE = 1.0 / math.sqrt(HEAD_DIM)
LOG2E = math.log2(math.e)
MESH = pl.DeviceIdType.MESH
F32 = jnp.float32
BF16 = jnp.bfloat16


def order(d):
    return jnp.where(d == 2, 3, jnp.where(d == 3, 2, d))


def y_of(p, j):
    return lax.rem(p // 2 + j, 4)


def dot(a, b):
    return jnp.dot(a, b, preferred_element_type=F32)


def dot_nt(a, b):
    return lax.dot_general(a, b, (((1,), (1,)), ((), ())), preferred_element_type=F32)


def kernel(
    q_in, k_in, v_in, g_in,
    dq_rx, dk_rx, dv_rx,
    kb, vb, xr, via, qgb, kt, vt, qt, gt, qft, gft,
    s0, s1, prob, ot, stat_tx, stat_rx, rows, dqt, dk_acc, dv_acc,
    dq_tx, sib_tx, sib_rx, kv_tx, yr,
    k_rs, v_rs, xr_rs, via_rs, qg_rs, st_rs, sib_rs, dq_rs, kv_rs, yr_rs,
    home_ss, xr_ss, self_s, fwd_ss, hop_ss, st_ss, sib_ss, dq_ss, kv_ss, yr_ss,
):
    r, col, g = lax.axis_index("row"), lax.axis_index("col"), lax.axis_index("head")
    y, c = r // 2, lax.rem(r, 2)
    xh, z = col // 4, lax.rem(col, 4)
    jw = lax.rem(y + z // 2, 2)
    pw = z + 4 * (lax.rem(y - jw + 4, 4) // 2)
    aw = lax.rem(pw, 2)
    pk, pq = r, col
    partner = (y, c, 1 - xh, z)
    sibling = (y, 1 - c, xh, z)
    relay = c == aw

    up, down = lax.rem(xh + g, 2), lax.rem(xh + 1 - g, 2)

    def dev(t):
        yy, cc, xx, zz = t[:4]
        return (2 * yy + cc, 4 * xx + zz, g if len(t) == 4 else t[4])

    def is_me(t):
        yy, cc, xx, zz = t
        return jnp.logical_and(2 * yy + cc == r, 4 * xx + zz == col)

    barrier = pltpu.get_barrier_semaphore()
    greeted = [partner, sibling] + [(y, c, xx, z, 1 - g) for xx in (up, down)]
    greeted += [(lax.rem(y + d, 4), c, xh, z) for d in (1, 2, 3)]
    greeted += [(y_of(pk, j), cc, xh, lax.rem(pk, 4)) for j in range(2) for cc in range(2)]
    greeted += [(pw // 2, aw, xh, lax.rem(z + d, 4)) for d in range(4)]
    greeted += [(y, cc, xh, lax.rem(z + d, 4)) for d in (1, 2, 3) for cc in range(2)]
    greeted += [(lax.rem(y + d, 4), c, pw // 4, lax.rem(pw, 4)) for d in range(4)]
    greeted += [(y_of(pq, j), c, xx, z) for j in range(2) for xx in range(2)]
    for t in greeted:
        pl.semaphore_signal(barrier, inc=1, device_id=dev(t), device_id_type=MESH)
    pl.semaphore_wait(barrier, len(greeted))

    def remote(src, dst, t, ssem, rsem):
        return pltpu.make_async_remote_copy(
            src_ref=src, dst_ref=dst, send_sem=ssem, recv_sem=rsem, device_id=dev(t), device_id_type=MESH
        )

    def put(src, dst, t, ssem, rsem):
        me = is_me(t)

        @pl.when(jnp.logical_not(me))
        def _():
            remote(src, dst, t, ssem, rsem).start()

        @pl.when(me)
        def _():
            pltpu.make_async_copy(src, dst, rsem).start()

    def sent(src, dst, t, ssem, rsem):
        @pl.when(jnp.logical_not(is_me(t)))
        def _():
            remote(src, dst, t, ssem, rsem).wait_send()

    def arrived(dst, rsem):
        pltpu.make_async_copy(dst, dst, rsem).wait()

    def cols(j):
        return pl.ds(j * HEAD_DIM, HEAD_DIM)

    def spread(arr, ref):
        out = []
        for j, xx in enumerate((up, down)):
            slot = y_of(pq, j)
            pltpu.make_async_copy(ref.at[:, cols(j)], via.at[arr, slot], via_rs.at[arr, slot]).start()
            t = (y, c, xx, z, 1 - g)
            out.append(remote(ref.at[:, cols(j)], xr.at[arr, j], t, home_ss.at[arr, j], xr_rs.at[arr, j]))
            out[-1].start()
        return out

    def cross(arr):
        out = []
        for j, (origin, xx) in enumerate(((down, up), (up, down))):
            slot = y_of(4 * origin + z, j)
            arrived(xr.at[arr, j], xr_rs.at[arr, j])
            out.append(
                remote(xr.at[arr, j], via.at[arr, slot], (y, c, xx, z, 1 - g), xr_ss.at[arr, j], via_rs.at[arr, slot])
            )
            out[-1].start()
        return out

    def hop(arr):
        out = []
        for n, d in enumerate((1, 3, 2)):
            to = lax.rem(y + d, 4)
            slot = {3: 1, 1: 2, 2: 3}[d]
            arrived(via.at[arr, to], via_rs.at[arr, to])
            out.append(
                remote(via.at[arr, to], qgb.at[arr, slot - 1], (to, c, xh, z), hop_ss.at[arr, n], qg_rs.at[arr, slot - 1])
            )
            out[-1].start()
        return out

    def home_kv(arr, j):
        ref, buf, sem = ((k_in, kb, k_rs), (v_in, vb, v_rs))[arr]
        slot = order(lax.rem(z - lax.rem(pk, 4) + 4, 4))
        t = (y_of(pk, j), c, xh, lax.rem(pk, 4))
        return (ref.at[:, cols(j)], buf.at[slot], t, self_s.at[arr, j], sem.at[slot])

    def forward_kv(arr, n):
        buf, sem = ((kb, k_rs), (vb, v_rs))[arr]
        return remote(buf.at[n], buf.at[n], sibling, fwd_ss.at[arr, n], sem.at[n])

    pending = spread(0, q_in)
    for arr in range(2):
        for j in range(2):
            put(*home_kv(arr, j))
    pending += spread(1, g_in)
    pending += cross(0)
    arrived(via.at[0, y], via_rs.at[0, y])
    qt[0] = via[0, y].T
    pending += hop(0)

    sbuf = (s0, s1)

    def scores(i, n, buf, m):
        s = dot(kb[n], qt[i])
        sbuf[buf][n] = s
        return jnp.maximum(m, jnp.max(s.reshape(BLK // 8, 8, BLK), axis=0))

    lowest = jnp.full((8, BLK), -jnp.inf, F32)
    def first_scores(n, m):
        arrived(kb.at[n], k_rs.at[n])

        @pl.when(relay)
        def _():
            forward_kv(0, n).start()

        kt[n] = kb[n].T
        return scores(0, n, 0, m)

    mx = lax.fori_loop(0, NB, first_scores, lowest)

    def fetch_v(n, carry):
        arrived(vb.at[n], v_rs.at[n])

        @pl.when(relay)
        def _():
            forward_kv(1, n).start()

        vt[n, :HEAD_DIM, :] = vb[n].T
        vt[n, HEAD_DIM:, :] = jnp.ones((AUG - HEAD_DIM, BLK), BF16)
        return carry

    lax.fori_loop(0, NB, fetch_v, 0)
    pending += cross(1)

    def weigh(i, n, buf, m):
        p = jnp.exp2((sbuf[buf][n] - m) * (SCALE * LOG2E)).astype(BF16)
        prob[i, n] = p
        ot[i] += dot(vt[n], p)

    def stat_copy(i):
        return remote(stat_tx.at[i], stat_rx.at[i], partner, st_ss.at[i], st_rs.at[i])

    def finish(i, m):
        if i == 0:
            arrived(via.at[1, y], via_rs.at[1, y])
            gt[0] = via[1, y].T
        else:
            arrived(qgb.at[1, i - 1], qg_rs.at[1, i - 1])
            gt[i] = qgb[1, i - 1].T
        stat_tx[i, 0:1] = m
        stat_tx[i, 1:2] = ot[i, HEAD_DIM : HEAD_DIM + 1]
        stat_tx[i, 2:3] = jnp.sum(gt[i].astype(F32) * ot[i, :HEAD_DIM], axis=0, keepdims=True)
        stat_copy(i).start()

    def forward(i, mx):
        buf = i % 2
        more = i + 1 < NB
        if more:
            arrived(qgb.at[0, i], qg_rs.at[0, i])
            qt[i + 1] = qgb[0, i].T
        m = jnp.max(mx, axis=0, keepdims=True)
        ot[i] = jnp.zeros((AUG, BLK), F32)

        def step(n, mx2):
            if more:
                mx2 = scores(i + 1, n, 1 - buf, mx2)
            weigh(i, n, buf, m)
            return mx2

        return m, lax.fori_loop(0, NB, step, lowest)

    def combine(i):
        stat_copy(i).wait()
        m0, l0, d0 = stat_tx[i, 0:1], stat_tx[i, 1:2], stat_tx[i, 2:3]
        m1, l1, d1 = stat_rx[i, 0:1], stat_rx[i, 1:2], stat_rx[i, 2:3]
        m = jnp.maximum(m0, m1)
        e0 = jnp.exp2((m0 - m) * (SCALE * LOG2E))
        e1 = jnp.exp2((m1 - m) * (SCALE * LOG2E))
        inv = 1.0 / (l0 * e0 + l1 * e1)
        f = e0 * inv
        rows[i, 0:1] = (d0 * e0 + d1 * e1) * inv
        rows[i, 1:2] = f * SCALE
        gft[i] = (gt[i].astype(F32) * f).astype(BF16)
        qft[i] = (qt[i].astype(F32) * (f * SCALE)).astype(BF16)
        dqt[i] = jnp.zeros((HEAD_DIM, BLK), F32)

    dk_acc[...] = jnp.zeros_like(dk_acc)
    dv_acc[...] = jnp.zeros_like(dv_acc)

    def dq_args(i):
        t = (lax.rem(y + order(i), 4), c, pw // 4, lax.rem(pw, 4))
        return (dq_tx.at[i], dq_rx.at[jw, xh], t, dq_ss.at[i], dq_rs.at[jw, xh])

    def sib_copy(n):
        return remote(sib_tx.at[n], sib_rx.at[n], sibling, sib_ss.at[n], sib_rs.at[n])

    def kv_args(n, raw):
        t = (y, aw, xh, lax.rem(z + order(n), 4))
        return [
            (kv_tx.at[n], raw.at[:, cols(0)], t, kv_ss.at[n], kv_rs.at[c, 0]),
            (kv_tx.at[n], yr.at[c], t, kv_ss.at[n], yr_rs.at[c]),
        ]

    def relay_down(arr):
        raw = (dk_rx, dv_rx)[arr]
        t = (lax.rem(y + 3, 4), c, xh, z)
        return remote(yr.at[arr], raw.at[:, cols(1)], t, yr_ss.at[arr], kv_rs.at[arr, 1])

    def by_core(run):
        @pl.when(c == 0)
        def _():
            run(dk_acc, dv_acc, dk_rx)

        @pl.when(c == 1)
        def _():
            run(dv_acc, dk_acc, dv_rx)

    def by_member(run):
        for j in range(2):

            @pl.when(jw == j)
            def _():
                run(j)

    def trade_kv(n):
        def run(_, other, __):
            sib_tx[n] = other[n].astype(BF16)

        by_core(run)
        sib_copy(n).start()

    def reduce_kv(n):
        arrived(sib_rx.at[n], sib_rs.at[n])

        def run(own, _, raw):
            kv_tx[n] = (own[n] + sib_rx[n].astype(F32)).astype(BF16)
            by_member(lambda j: put(*kv_args(n, raw)[j]))

        by_core(run)

    def backward(i, n):
        p = prob[i, n]
        dp = dot(vb[n], gt[i])
        ds = (p.astype(F32) * (dp - rows[i, 0:1])).astype(BF16)
        dv_acc[n] += dot_nt(p, gft[i])
        dk_acc[n] += dot_nt(ds, qft[i])
        dqt[i] += dot(kt[n], ds)

    def send_dq(i):
        dq_tx[i] = (dqt[i] * rows[i, 1:2]).T.astype(BF16)
        put(*dq_args(i))

    def loop(lo, hi, body):
        def run(n, carry):
            body(n)
            return carry

        lax.fori_loop(lo, hi, run, 0)

    peaks = []
    for i in range(NB):
        m, mx = forward(i, mx)
        peaks.append(m)
        if i == 0:
            pending += hop(1)
        if i == 2:
            finish(0, peaks[0])
            finish(1, peaks[1])
    finish(2, peaks[2])
    finish(3, peaks[3])

    def early(i):
        def pair(n):
            backward(i, 2 * n)
            backward(i, 2 * n + 1)

        combine(i)
        loop(0, NB // 2, pair)
        send_dq(i)

    early(1)
    early(3)
    combine(2)
    combine(0)

    def both(n):
        backward(2, n)
        backward(0, n)
        trade_kv(n)

    loop(0, 2, both)
    reduce_kv(jnp.int32(0))
    backward(2, 2)
    backward(2, 3)
    send_dq(2)
    reduce_kv(jnp.int32(1))

    def final(n):
        backward(0, n)
        trade_kv(n)

    loop(2, 4, final)
    reduce_kv(jnp.int32(2))
    send_dq(0)
    reduce_kv(jnp.int32(3))
    for arr in range(2):
        arrived(yr.at[arr], yr_rs.at[arr])
        relay_down(arr).start()

    for j in range(2):
        for n in range(2):
            arrived(dq_rx.at[j, n], dq_rs.at[j, n])
        for arr, raw in ((0, dk_rx), (1, dv_rx)):
            arrived(raw.at[:, cols(j)], kv_rs.at[arr, j])

    for copy in pending:
        copy.wait_send()
    for arr in range(2):
        for j in range(2):
            sent(*home_kv(arr, j))

    @pl.when(relay)
    def _():
        for arr in range(2):
            for n in range(NB):
                forward_kv(arr, n).wait_send()

    for i in range(NB):
        sent(*dq_args(jnp.int32(i)))
        sent(*kv_args(jnp.int32(i), dk_rx)[0])
        sib_copy(i).wait_send()
    for arr in range(2):
        relay_down(arr).wait_send()


def collect(dq_raw, dk_raw, dv_raw, dq_out, dk_out, dv_out):
    for j in range(2):
        total = dq_raw[j, 0].astype(F32) + dq_raw[j, 1].astype(F32)
        dq_out[:, j * HEAD_DIM : (j + 1) * HEAD_DIM] = total.astype(BF16)
    dk_out[...] = dk_raw[...]
    dv_out[...] = dv_raw[...]


def per_device(queries, key_states, value_states, out_grad):
    rows, width = queries.shape
    shape = jax.ShapeDtypeStruct((rows, width), BF16)
    vm = pltpu.VMEM
    dma = pltpu.SemaphoreType.DMA
    tile = (NB, BLK, HEAD_DIM)
    tile_t = (NB, HEAD_DIM, BLK)
    flops = 6 * 2 * (NB * BLK) ** 2 * HEAD_DIM
    raw = pl.pallas_call(
        kernel,
        out_shape=(jax.ShapeDtypeStruct((2, 2, BLK, HEAD_DIM), BF16), shape, shape),
        in_specs=[pl.BlockSpec(memory_space=pl.ANY)] * 4,
        out_specs=tuple([pl.BlockSpec(memory_space=pl.ANY)] * 3),
        scratch_shapes=[
            vm(tile, BF16), vm(tile, BF16), vm((2, 2, BLK, HEAD_DIM), BF16), vm((2,) + tile, BF16), vm((2, NB - 1, BLK, HEAD_DIM), BF16),
            vm(tile_t, BF16), vm((NB, AUG, BLK), BF16), vm(tile_t, BF16), vm(tile_t, BF16),
            vm(tile_t, BF16), vm(tile_t, BF16),
            vm((NB, BLK, BLK), F32), vm((NB, BLK, BLK), F32), vm((NB, NB, BLK, BLK), BF16), vm((NB, AUG, BLK), F32),
            vm((NB, 8, BLK), F32), vm((NB, 8, BLK), F32), vm((NB, 8, BLK), F32), vm(tile_t, F32),
            vm(tile, F32), vm(tile, F32),
            vm(tile, BF16), vm(tile, BF16), vm(tile, BF16), vm(tile, BF16), vm((2, BLK, HEAD_DIM), BF16),
            dma((NB,)), dma((NB,)), dma((2, 2)), dma((2, NB)), dma((2, NB - 1)), dma((NB,)), dma((NB,)), dma((2, 2)), dma((2, 2)), dma((2,)),
            dma((2, 2)), dma((2, 2)), dma((2, 2)), dma((2, NB)), dma((2, 3)), dma((NB,)), dma((NB,)), dma((NB,)), dma((NB,)), dma((2,)),
        ],
        compiler_params=pltpu.CompilerParams(
            collective_id=0, has_side_effects=True, vmem_limit_bytes=62 * 1024 * 1024
        ),
        cost_estimate=pl.CostEstimate(flops=flops, bytes_accessed=4 * rows * width * 2, transcendentals=(NB * BLK) ** 2),
    )(queries, key_states, value_states, out_grad)
    part = rows // 3
    whole = pl.BlockSpec((part, width), lambda n: (n, 0))
    return pl.pallas_call(
        collect,
        out_shape=(shape, shape, shape),
        grid=(3,),
        in_specs=[pl.BlockSpec((2, 2, part, HEAD_DIM), lambda n: (0, 0, n, 0))] + [whole] * 2,
        out_specs=(whole,) * 3,
    )(*raw)


def solution(mesh):
    placed = (
        P("row", ("head", "col")),
        P("col", ("head", "row")),
        P("col", ("head", "row")),
        P("row", ("head", "col")),
    )
    return jax.shard_map(
        per_device,
        mesh=mesh,
        in_specs=placed,
        out_specs=(P("row", ("head", "col")), P("col", ("head", "row")), P("col", ("head", "row"))),
        check_vma=False,
    )
```

```python
import math

import jax
import jax.numpy as jnp
from jax import lax
from jax.experimental import pallas as pl
from jax.experimental.pallas import tpu as pltpu
from jax.sharding import PartitionSpec as P

HEAD_DIM = 128
BLK = 768
NB = 4
AUG = 144
SCALE = 1.0 / math.sqrt(HEAD_DIM)
LOG2E = math.log2(math.e)
MESH = pl.DeviceIdType.MESH
F32 = jnp.float32
BF16 = jnp.bfloat16


def order(d):
    return jnp.where(d == 2, 3, jnp.where(d == 3, 2, d))


def y_of(p, j):
    return lax.rem(p // 2 + j, 4)


def dot(a, b):
    return jnp.dot(a, b, preferred_element_type=F32)


def dot_nt(a, b):
    return lax.dot_general(a, b, (((1,), (1,)), ((), ())), preferred_element_type=F32)


def kernel(
    q_in, k_in, v_in, g_in,
    dq_rx, dk_rx, dv_rx,
    kb, vb, xr, via, qgb, kt, vt, qt, gt, qft, gft,
    s0, s1, prob, ot, stat_tx, stat_rx, rows, dqt, dk_acc, dv_acc,
    dq_tx, sib_tx, sib_rx, kv_tx, yr,
    k_rs, v_rs, xr_rs, via_rs, qg_rs, st_rs, sib_rs, dq_rs, kv_rs, yr_rs,
    home_ss, xr_ss, self_s, fwd_ss, hop_ss, st_ss, sib_ss, dq_ss, kv_ss, yr_ss,
):
    r, col, g = lax.axis_index("row"), lax.axis_index("col"), lax.axis_index("head")
    y, c = r // 2, lax.rem(r, 2)
    xh, z = col // 4, lax.rem(col, 4)
    jw = lax.rem(y + z // 2, 2)
    pw = z + 4 * (lax.rem(y - jw + 4, 4) // 2)
    aw = lax.rem(pw, 2)
    pk, pq = r, col
    partner = (y, c, 1 - xh, z)
    sibling = (y, 1 - c, xh, z)
    relay = c == aw

    up, down = lax.rem(xh + g, 2), lax.rem(xh + 1 - g, 2)

    def dev(t):
        yy, cc, xx, zz = t[:4]
        return (2 * yy + cc, 4 * xx + zz, g if len(t) == 4 else t[4])

    def is_me(t):
        yy, cc, xx, zz = t
        return jnp.logical_and(2 * yy + cc == r, 4 * xx + zz == col)

    barrier = pltpu.get_barrier_semaphore()
    greeted = [partner, sibling] + [(y, c, xx, z, 1 - g) for xx in (up, down)]
    greeted += [(lax.rem(y + d, 4), c, xh, z) for d in (1, 2, 3)]
    greeted += [(y_of(pk, j), cc, xh, lax.rem(pk, 4)) for j in range(2) for cc in range(2)]
    greeted += [(pw // 2, aw, xh, lax.rem(z + d, 4)) for d in range(4)]
    greeted += [(y, cc, xh, lax.rem(z + d, 4)) for d in (1, 2, 3) for cc in range(2)]
    greeted += [(lax.rem(y + d, 4), c, pw // 4, lax.rem(pw, 4)) for d in range(4)]
    greeted += [(y_of(pq, j), c, xx, z) for j in range(2) for xx in range(2)]
    for t in greeted:
        pl.semaphore_signal(barrier, inc=1, device_id=dev(t), device_id_type=MESH)
    pl.semaphore_wait(barrier, len(greeted))

    def remote(src, dst, t, ssem, rsem):
        return pltpu.make_async_remote_copy(
            src_ref=src, dst_ref=dst, send_sem=ssem, recv_sem=rsem, device_id=dev(t), device_id_type=MESH
        )

    def put(src, dst, t, ssem, rsem):
        me = is_me(t)

        @pl.when(jnp.logical_not(me))
        def _():
            remote(src, dst, t, ssem, rsem).start()

        @pl.when(me)
        def _():
            pltpu.make_async_copy(src, dst, rsem).start()

    def sent(src, dst, t, ssem, rsem):
        @pl.when(jnp.logical_not(is_me(t)))
        def _():
            remote(src, dst, t, ssem, rsem).wait_send()

    def arrived(dst, rsem):
        pltpu.make_async_copy(dst, dst, rsem).wait()

    def cols(j):
        return pl.ds(j * HEAD_DIM, HEAD_DIM)

    def spread(arr, ref):
        out = []
        for j, xx in enumerate((up, down)):
            slot = y_of(pq, j)
            pltpu.make_async_copy(ref.at[:, cols(j)], via.at[arr, slot], via_rs.at[arr, slot]).start()
            t = (y, c, xx, z, 1 - g)
            out.append(remote(ref.at[:, cols(j)], xr.at[arr, j], t, home_ss.at[arr, j], xr_rs.at[arr, j]))
            out[-1].start()
        return out

    def cross(arr):
        out = []
        for j, (origin, xx) in enumerate(((down, up), (up, down))):
            slot = y_of(4 * origin + z, j)
            arrived(xr.at[arr, j], xr_rs.at[arr, j])
            out.append(
                remote(xr.at[arr, j], via.at[arr, slot], (y, c, xx, z, 1 - g), xr_ss.at[arr, j], via_rs.at[arr, slot])
            )
            out[-1].start()
        return out

    def hop(arr):
        out = []
        for n, d in enumerate((1, 3, 2)):
            to = lax.rem(y + d, 4)
            slot = {3: 1, 1: 2, 2: 3}[d]
            arrived(via.at[arr, to], via_rs.at[arr, to])
            out.append(
                remote(via.at[arr, to], qgb.at[arr, slot - 1], (to, c, xh, z), hop_ss.at[arr, n], qg_rs.at[arr, slot - 1])
            )
            out[-1].start()
        return out

    def home_kv(arr, j):
        ref, buf, sem = ((k_in, kb, k_rs), (v_in, vb, v_rs))[arr]
        slot = order(lax.rem(z - lax.rem(pk, 4) + 4, 4))
        t = (y_of(pk, j), c, xh, lax.rem(pk, 4))
        return (ref.at[:, cols(j)], buf.at[slot], t, self_s.at[arr, j], sem.at[slot])

    def forward_kv(arr, n):
        buf, sem = ((kb, k_rs), (vb, v_rs))[arr]
        return remote(buf.at[n], buf.at[n], sibling, fwd_ss.at[arr, n], sem.at[n])

    pending = spread(0, q_in)
    for arr in range(2):
        for j in range(2):
            put(*home_kv(arr, j))
    pending += spread(1, g_in)
    pending += cross(0)
    arrived(via.at[0, y], via_rs.at[0, y])
    qt[0] = via[0, y].T
    pending += hop(0)

    sbuf = (s0, s1)

    def scores(i, n, buf, m):
        s = dot(kb[n], qt[i])
        sbuf[buf][n] = s
        return jnp.maximum(m, jnp.max(s.reshape(BLK // 8, 8, BLK), axis=0))

    lowest = jnp.full((8, BLK), -jnp.inf, F32)
    def first_scores(n, m):
        arrived(kb.at[n], k_rs.at[n])

        @pl.when(relay)
        def _():
            forward_kv(0, n).start()

        kt[n] = kb[n].T
        return scores(0, n, 0, m)

    mx = lax.fori_loop(0, NB, first_scores, lowest)

    def fetch_v(n, carry):
        arrived(vb.at[n], v_rs.at[n])

        @pl.when(relay)
        def _():
            forward_kv(1, n).start()

        vt[n, :HEAD_DIM, :] = vb[n].T
        vt[n, HEAD_DIM:, :] = jnp.ones((AUG - HEAD_DIM, BLK), BF16)
        return carry

    lax.fori_loop(0, NB, fetch_v, 0)
    pending += cross(1)

    def weigh(i, n, buf, m):
        p = jnp.exp2((sbuf[buf][n] - m) * (SCALE * LOG2E)).astype(BF16)
        prob[i, n] = p
        ot[i] += dot(vt[n], p)

    def stat_copy(i):
        return remote(stat_tx.at[i], stat_rx.at[i], partner, st_ss.at[i], st_rs.at[i])

    def finish(i, m):
        if i == 0:
            arrived(via.at[1, y], via_rs.at[1, y])
            gt[0] = via[1, y].T
        else:
            arrived(qgb.at[1, i - 1], qg_rs.at[1, i - 1])
            gt[i] = qgb[1, i - 1].T
        stat_tx[i, 0:1] = m
        stat_tx[i, 1:2] = ot[i, HEAD_DIM : HEAD_DIM + 1]
        stat_tx[i, 2:3] = jnp.sum(gt[i].astype(F32) * ot[i, :HEAD_DIM], axis=0, keepdims=True)
        stat_copy(i).start()

    def forward(i, mx):
        buf = i % 2
        more = i + 1 < NB
        if more:
            arrived(qgb.at[0, i], qg_rs.at[0, i])
            qt[i + 1] = qgb[0, i].T
        m = jnp.max(mx, axis=0, keepdims=True)
        ot[i] = jnp.zeros((AUG, BLK), F32)

        def step(n, mx2):
            if more:
                mx2 = scores(i + 1, n, 1 - buf, mx2)
            weigh(i, n, buf, m)
            return mx2

        return m, lax.fori_loop(0, NB, step, lowest)

    def combine(i):
        stat_copy(i).wait()
        m0, l0, d0 = stat_tx[i, 0:1], stat_tx[i, 1:2], stat_tx[i, 2:3]
        m1, l1, d1 = stat_rx[i, 0:1], stat_rx[i, 1:2], stat_rx[i, 2:3]
        m = jnp.maximum(m0, m1)
        e0 = jnp.exp2((m0 - m) * (SCALE * LOG2E))
        e1 = jnp.exp2((m1 - m) * (SCALE * LOG2E))
        inv = 1.0 / (l0 * e0 + l1 * e1)
        f = e0 * inv
        rows[i, 0:1] = (d0 * e0 + d1 * e1) * inv
        rows[i, 1:2] = f * SCALE
        gft[i] = (gt[i].astype(F32) * f).astype(BF16)
        qft[i] = (qt[i].astype(F32) * (f * SCALE)).astype(BF16)
        dqt[i] = jnp.zeros((HEAD_DIM, BLK), F32)

    dk_acc[...] = jnp.zeros_like(dk_acc)
    dv_acc[...] = jnp.zeros_like(dv_acc)

    def dq_args(i):
        t = (lax.rem(y + order(i), 4), c, pw // 4, lax.rem(pw, 4))
        return (dq_tx.at[i], dq_rx.at[jw, xh], t, dq_ss.at[i], dq_rs.at[jw, xh])

    def sib_copy(n):
        return remote(sib_tx.at[n], sib_rx.at[n], sibling, sib_ss.at[n], sib_rs.at[n])

    def kv_args(n, raw):
        t = (y, aw, xh, lax.rem(z + order(n), 4))
        return [
            (kv_tx.at[n], raw.at[:, cols(0)], t, kv_ss.at[n], kv_rs.at[c, 0]),
            (kv_tx.at[n], yr.at[c], t, kv_ss.at[n], yr_rs.at[c]),
        ]

    def relay_down(arr):
        raw = (dk_rx, dv_rx)[arr]
        t = (lax.rem(y + 3, 4), c, xh, z)
        return remote(yr.at[arr], raw.at[:, cols(1)], t, yr_ss.at[arr], kv_rs.at[arr, 1])

    def by_core(run):
        @pl.when(c == 0)
        def _():
            run(dk_acc, dv_acc, dk_rx)

        @pl.when(c == 1)
        def _():
            run(dv_acc, dk_acc, dv_rx)

    def by_member(run):
        for j in range(2):

            @pl.when(jw == j)
            def _():
                run(j)

    def trade_kv(n):
        def run(_, other, __):
            sib_tx[n] = other[n].astype(BF16)

        by_core(run)
        sib_copy(n).start()

    def reduce_kv(n):
        arrived(sib_rx.at[n], sib_rs.at[n])

        def run(own, _, raw):
            kv_tx[n] = (own[n] + sib_rx[n].astype(F32)).astype(BF16)
            by_member(lambda j: put(*kv_args(n, raw)[j]))

        by_core(run)

    def backward(i, n):
        p = prob[i, n]
        dp = dot(vb[n], gt[i])
        ds = (p.astype(F32) * (dp - rows[i, 0:1])).astype(BF16)
        dv_acc[n] += dot_nt(p, gft[i])
        dk_acc[n] += dot_nt(ds, qft[i])
        dqt[i] += dot(kt[n], ds)

    def send_dq(i):
        dq_tx[i] = (dqt[i] * rows[i, 1:2]).T.astype(BF16)
        put(*dq_args(i))

    def loop(lo, hi, body):
        def run(n, carry):
            body(n)
            return carry

        lax.fori_loop(lo, hi, run, 0)

    peaks = []
    for i in range(NB):
        m, mx = forward(i, mx)
        peaks.append(m)
        if i == 0:
            pending += hop(1)
        if i == 2:
            finish(0, peaks[0])
            finish(1, peaks[1])
    finish(2, peaks[2])
    finish(3, peaks[3])

    def early(i):
        def pair(n):
            backward(i, 2 * n)
            backward(i, 2 * n + 1)

        combine(i)
        loop(0, NB // 2, pair)
        send_dq(i)

    loop(0, 2, lambda t: early(1 + 2 * t))
    combine(2)
    combine(0)

    def both(t):
        n = 3 - 2 * t
        backward(2, n)
        backward(0, n)
        trade_kv(n)

    def relay_now():
        for arr in range(2):
            arrived(yr.at[arr], yr_rs.at[arr])
            relay_down(arr).start()

    passed = order(lax.rem(z - 2 * lax.rem(y + 1, 2) - c + 4, 4))

    loop(0, 2, both)
    reduce_kv(jnp.int32(3))
    backward(2, 2)
    backward(2, 0)
    send_dq(2)
    reduce_kv(jnp.int32(1))

    def final(t):
        pl.when(passed == 3 - 2 * t)(relay_now)
        n = 2 - 2 * t
        backward(0, n)
        trade_kv(n)

    loop(0, 2, final)
    reduce_kv(jnp.int32(2))
    send_dq(0)
    reduce_kv(jnp.int32(0))
    pl.when(lax.rem(passed, 2) == 0)(relay_now)

    for j in range(2):
        for n in range(2):
            arrived(dq_rx.at[j, n], dq_rs.at[j, n])
        for arr, raw in ((0, dk_rx), (1, dv_rx)):
            arrived(raw.at[:, cols(j)], kv_rs.at[arr, j])

    for copy in pending:
        copy.wait_send()
    for arr in range(2):
        for j in range(2):
            sent(*home_kv(arr, j))

    @pl.when(relay)
    def _():
        for arr in range(2):
            for n in range(NB):
                forward_kv(arr, n).wait_send()

    for i in range(NB):
        sent(*dq_args(jnp.int32(i)))
        sent(*kv_args(jnp.int32(i), dk_rx)[0])
        sib_copy(i).wait_send()
    for arr in range(2):
        relay_down(arr).wait_send()


def collect(dq_raw, dk_raw, dv_raw, dq_out, dk_out, dv_out):
    for j in range(2):
        total = dq_raw[j, 0].astype(F32) + dq_raw[j, 1].astype(F32)
        dq_out[:, j * HEAD_DIM : (j + 1) * HEAD_DIM] = total.astype(BF16)
    dk_out[...] = dk_raw[...]
    dv_out[...] = dv_raw[...]


def per_device(queries, key_states, value_states, out_grad):
    rows, width = queries.shape
    shape = jax.ShapeDtypeStruct((rows, width), BF16)
    vm = pltpu.VMEM
    dma = pltpu.SemaphoreType.DMA
    tile = (NB, BLK, HEAD_DIM)
    tile_t = (NB, HEAD_DIM, BLK)
    flops = 6 * 2 * (NB * BLK) ** 2 * HEAD_DIM
    raw = pl.pallas_call(
        kernel,
        out_shape=(jax.ShapeDtypeStruct((2, 2, BLK, HEAD_DIM), BF16), shape, shape),
        in_specs=[pl.BlockSpec(memory_space=pl.ANY)] * 4,
        out_specs=tuple([pl.BlockSpec(memory_space=pl.ANY)] * 3),
        scratch_shapes=[
            vm(tile, BF16), vm(tile, BF16), vm((2, 2, BLK, HEAD_DIM), BF16), vm((2,) + tile, BF16), vm((2, NB - 1, BLK, HEAD_DIM), BF16),
            vm(tile_t, BF16), vm((NB, AUG, BLK), BF16), vm(tile_t, BF16), vm(tile_t, BF16),
            vm(tile_t, BF16), vm(tile_t, BF16),
            vm((NB, BLK, BLK), F32), vm((NB, BLK, BLK), F32), vm((NB, NB, BLK, BLK), BF16), vm((NB, AUG, BLK), F32),
            vm((NB, 8, BLK), F32), vm((NB, 8, BLK), F32), vm((NB, 8, BLK), F32), vm(tile_t, F32),
            vm(tile, F32), vm(tile, F32),
            vm(tile, BF16), vm(tile, BF16), vm(tile, BF16), vm(tile, BF16), vm((2, BLK, HEAD_DIM), BF16),
            dma((NB,)), dma((NB,)), dma((2, 2)), dma((2, NB)), dma((2, NB - 1)), dma((NB,)), dma((NB,)), dma((2, 2)), dma((2, 2)), dma((2,)),
            dma((2, 2)), dma((2, 2)), dma((2, 2)), dma((2, NB)), dma((2, 3)), dma((NB,)), dma((NB,)), dma((NB,)), dma((NB,)), dma((2,)),
        ],
        compiler_params=pltpu.CompilerParams(
            collective_id=0, has_side_effects=True, vmem_limit_bytes=62 * 1024 * 1024
        ),
        cost_estimate=pl.CostEstimate(flops=flops, bytes_accessed=4 * rows * width * 2, transcendentals=(NB * BLK) ** 2),
    )(queries, key_states, value_states, out_grad)
    whole = pl.BlockSpec(memory_space=pltpu.VMEM)
    return pl.pallas_call(
        collect,
        out_shape=(shape, shape, shape),
        in_specs=[whole] * 3,
        out_specs=(whole,) * 3,
    )(*raw)


def solution(mesh):
    placed = (
        P("row", ("head", "col")),
        P("col", ("head", "row")),
        P("col", ("head", "row")),
        P("row", ("head", "col")),
    )
    return jax.shard_map(
        per_device,
        mesh=mesh,
        in_specs=placed,
        out_specs=(P("row", ("head", "col")), P("col", ("head", "row")), P("col", ("head", "row"))),
        check_vma=False,
    )
```

```python
import math

import jax
import jax.numpy as jnp
from jax import lax
from jax.experimental import pallas as pl
from jax.experimental.pallas import tpu as pltpu
from jax.sharding import PartitionSpec as P

HEAD_DIM = 128
BLK = 768
NB = 4
AUG = 144
SCALE = 1.0 / math.sqrt(HEAD_DIM)
LOG2E = math.log2(math.e)
MESH = pl.DeviceIdType.MESH
F32 = jnp.float32
BF16 = jnp.bfloat16


def order(d):
    return jnp.where(d == 2, 3, jnp.where(d == 3, 2, d))


def y_of(p, j):
    return lax.rem(p // 2 + j, 4)


def dot(a, b):
    return jnp.dot(a, b, preferred_element_type=F32)


def dot_nt(a, b):
    return lax.dot_general(a, b, (((1,), (1,)), ((), ())), preferred_element_type=F32)


def kernel(
    q_in, k_in, v_in, g_in,
    dq_rx, dk_rx, dv_rx,
    kb, vb, xr, via, qgb, kt, vt, qt, gt, qft, gft,
    s0, s1, prob, ot, stat_tx, stat_rx, rows, dqt, dk_acc, dv_acc,
    dq_tx, sib_tx, sib_rx, kv_tx, yr,
    k_rs, v_rs, xr_rs, via_rs, qg_rs, st_rs, sib_rs, dq_rs, kv_rs, yr_rs,
    home_ss, xr_ss, self_s, fwd_ss, hop_ss, st_ss, sib_ss, dq_ss, kv_ss, yr_ss,
):
    r, col, g = lax.axis_index("row"), lax.axis_index("col"), lax.axis_index("head")
    y, c = r // 2, lax.rem(r, 2)
    xh, z = col // 4, lax.rem(col, 4)
    jw = lax.rem(y + z // 2, 2)
    pw = z + 4 * (lax.rem(y - jw + 4, 4) // 2)
    aw = lax.rem(pw, 2)
    pk, pq = r, col
    partner = (y, c, 1 - xh, z)
    sibling = (y, 1 - c, xh, z)
    relay = c == aw

    up, down = lax.rem(xh + g, 2), lax.rem(xh + 1 - g, 2)

    def dev(t):
        yy, cc, xx, zz = t[:4]
        return (2 * yy + cc, 4 * xx + zz, g if len(t) == 4 else t[4])

    def is_me(t):
        yy, cc, xx, zz = t
        return jnp.logical_and(2 * yy + cc == r, 4 * xx + zz == col)

    barrier = pltpu.get_barrier_semaphore()
    greeted = [partner, sibling] + [(y, c, xx, z, 1 - g) for xx in (up, down)]
    greeted += [(lax.rem(y + d, 4), c, xh, z) for d in (1, 2, 3)]
    greeted += [(y_of(pk, j), cc, xh, lax.rem(pk, 4)) for j in range(2) for cc in range(2)]
    greeted += [(pw // 2, aw, xh, lax.rem(z + d, 4)) for d in range(4)]
    greeted += [(y, cc, xh, lax.rem(z + d, 4)) for d in (1, 2, 3) for cc in range(2)]
    greeted += [(lax.rem(y + d, 4), c, pw // 4, lax.rem(pw, 4)) for d in range(4)]
    greeted += [(y_of(pq, j), c, xx, z) for j in range(2) for xx in range(2)]
    for t in greeted:
        pl.semaphore_signal(barrier, inc=1, device_id=dev(t), device_id_type=MESH)
    pl.semaphore_wait(barrier, len(greeted))

    def remote(src, dst, t, ssem, rsem):
        return pltpu.make_async_remote_copy(
            src_ref=src, dst_ref=dst, send_sem=ssem, recv_sem=rsem, device_id=dev(t), device_id_type=MESH
        )

    def put(src, dst, t, ssem, rsem):
        me = is_me(t)

        @pl.when(jnp.logical_not(me))
        def _():
            remote(src, dst, t, ssem, rsem).start()

        @pl.when(me)
        def _():
            pltpu.make_async_copy(src, dst, rsem).start()

    def sent(src, dst, t, ssem, rsem):
        @pl.when(jnp.logical_not(is_me(t)))
        def _():
            remote(src, dst, t, ssem, rsem).wait_send()

    def arrived(dst, rsem):
        pltpu.make_async_copy(dst, dst, rsem).wait()

    def cols(j):
        return pl.ds(j * HEAD_DIM, HEAD_DIM)

    def spread(arr, ref):
        out = []
        for j, xx in enumerate((up, down)):
            slot = y_of(pq, j)
            pltpu.make_async_copy(ref.at[:, cols(j)], via.at[arr, slot], via_rs.at[arr, slot]).start()
            t = (y, c, xx, z, 1 - g)
            out.append(remote(ref.at[:, cols(j)], xr.at[arr, j], t, home_ss.at[arr, j], xr_rs.at[arr, j]))
            out[-1].start()
        return out

    def cross(arr):
        out = []
        for j, (origin, xx) in enumerate(((down, up), (up, down))):
            slot = y_of(4 * origin + z, j)
            arrived(xr.at[arr, j], xr_rs.at[arr, j])
            out.append(
                remote(xr.at[arr, j], via.at[arr, slot], (y, c, xx, z, 1 - g), xr_ss.at[arr, j], via_rs.at[arr, slot])
            )
            out[-1].start()
        return out

    def hop_copy(arr, n):
        d = (1, 3, 2)[n]
        to = lax.rem(y + d, 4)
        slot = {3: 1, 1: 2, 2: 3}[d] - 1
        return remote(via.at[arr, to], qgb.at[arr, slot], (to, c, xh, z), hop_ss.at[arr, n], qg_rs.at[arr, slot])

    def hop(arr, n):
        to = lax.rem(y + (1, 3, 2)[n], 4)
        arrived(via.at[arr, to], via_rs.at[arr, to])
        hop_copy(arr, n).start()

    def home_kv(arr, j):
        ref, buf, sem = ((k_in, kb, k_rs), (v_in, vb, v_rs))[arr]
        slot = order(lax.rem(z - lax.rem(pk, 4) + 4, 4))
        t = (y_of(pk, j), c, xh, lax.rem(pk, 4))
        return (ref.at[:, cols(j)], buf.at[slot], t, self_s.at[arr, j], sem.at[slot])

    def forward_kv(arr, n):
        buf, sem = ((kb, k_rs), (vb, v_rs))[arr]
        return remote(buf.at[n], buf.at[n], sibling, fwd_ss.at[arr, n], sem.at[n])

    pending = spread(0, q_in)
    for arr in range(2):
        for j in range(2):
            put(*home_kv(arr, j))
    pending += spread(1, g_in)
    pending += cross(0)
    arrived(via.at[0, y], via_rs.at[0, y])
    qt[0] = via[0, y].T
    for n in range(3):
        hop(0, n)
    pending += [hop_copy(arr, n) for arr in range(2) for n in range(3)]

    sbuf = (s0, s1)

    def scores(i, n, buf, m):
        s = dot(kb[n], qt[i])
        sbuf[buf][n] = s
        return jnp.maximum(m, jnp.max(s.reshape(BLK // 8, 8, BLK), axis=0))

    lowest = jnp.full((8, BLK), -jnp.inf, F32)
    def first_scores(n, m):
        arrived(kb.at[n], k_rs.at[n])

        @pl.when(relay)
        def _():
            forward_kv(0, n).start()

        kt[n] = kb[n].T
        return scores(0, n, 0, m)

    mx = lax.fori_loop(0, NB, first_scores, lowest)

    def fetch_v(n):
        arrived(vb.at[n], v_rs.at[n])

        @pl.when(relay)
        def _():
            forward_kv(1, n).start()

        vt[n, :HEAD_DIM, :] = vb[n].T
        vt[n, HEAD_DIM:, :] = jnp.ones((AUG - HEAD_DIM, BLK), BF16)

    def weigh(i, n, buf, m):
        p = jnp.exp2((sbuf[buf][n] - m) * (SCALE * LOG2E)).astype(BF16)
        prob[i, n] = p
        ot[i] += dot(vt[n], p)

    def stat_copy(i):
        return remote(stat_tx.at[i], stat_rx.at[i], partner, st_ss.at[i], st_rs.at[i])

    def finish(i, m):
        if i == 0:
            arrived(via.at[1, y], via_rs.at[1, y])
            gt[0] = via[1, y].T
        else:
            arrived(qgb.at[1, i - 1], qg_rs.at[1, i - 1])
            gt[i] = qgb[1, i - 1].T
        stat_tx[i, 0:1] = m
        stat_tx[i, 1:2] = ot[i, HEAD_DIM : HEAD_DIM + 1]
        stat_tx[i, 2:3] = jnp.sum(gt[i].astype(F32) * ot[i, :HEAD_DIM], axis=0, keepdims=True)
        stat_copy(i).start()

    def forward(i, mx):
        buf = i % 2
        more = i + 1 < NB
        if more:
            arrived(qgb.at[0, i], qg_rs.at[0, i])
            qt[i + 1] = qgb[0, i].T
        m = jnp.max(mx, axis=0, keepdims=True)
        ot[i] = jnp.zeros((AUG, BLK), F32)

        def step(n, mx2):
            if i == 0:
                fetch_v(n)
            if more:
                mx2 = scores(i + 1, n, 1 - buf, mx2)
            weigh(i, n, buf, m)
            if i == 0:
                for k in range(3):
                    pl.when(n == k + 1)(lambda: hop(1, k))
            return mx2

        return m, lax.fori_loop(0, NB, step, lowest)

    def combine(i):
        stat_copy(i).wait()
        m0, l0, d0 = stat_tx[i, 0:1], stat_tx[i, 1:2], stat_tx[i, 2:3]
        m1, l1, d1 = stat_rx[i, 0:1], stat_rx[i, 1:2], stat_rx[i, 2:3]
        m = jnp.maximum(m0, m1)
        e0 = jnp.exp2((m0 - m) * (SCALE * LOG2E))
        e1 = jnp.exp2((m1 - m) * (SCALE * LOG2E))
        inv = 1.0 / (l0 * e0 + l1 * e1)
        f = e0 * inv
        rows[i, 0:1] = (d0 * e0 + d1 * e1) * inv
        rows[i, 1:2] = f * SCALE
        gft[i] = (gt[i].astype(F32) * f).astype(BF16)
        qft[i] = (qt[i].astype(F32) * (f * SCALE)).astype(BF16)
        dqt[i] = jnp.zeros((HEAD_DIM, BLK), F32)

    dk_acc[...] = jnp.zeros_like(dk_acc)
    dv_acc[...] = jnp.zeros_like(dv_acc)

    def dq_args(i):
        t = (lax.rem(y + order(i), 4), c, pw // 4, lax.rem(pw, 4))
        return (dq_tx.at[i], dq_rx.at[jw, xh], t, dq_ss.at[i], dq_rs.at[jw, xh])

    def sib_copy(n):
        return remote(sib_tx.at[n], sib_rx.at[n], sibling, sib_ss.at[n], sib_rs.at[n])

    def kv_args(n, raw):
        t = (y, aw, xh, lax.rem(z + order(n), 4))
        return [
            (kv_tx.at[n], raw.at[:, cols(0)], t, kv_ss.at[n], kv_rs.at[c, 0]),
            (kv_tx.at[n], yr.at[c], t, kv_ss.at[n], yr_rs.at[c]),
        ]

    def relay_down(arr):
        raw = (dk_rx, dv_rx)[arr]
        t = (lax.rem(y + 3, 4), c, xh, z)
        return remote(yr.at[arr], raw.at[:, cols(1)], t, yr_ss.at[arr], kv_rs.at[arr, 1])

    def by_core(run):
        @pl.when(c == 0)
        def _():
            run(dk_acc, dv_acc, dk_rx)

        @pl.when(c == 1)
        def _():
            run(dv_acc, dk_acc, dv_rx)

    def by_member(run):
        for j in range(2):

            @pl.when(jw == j)
            def _():
                run(j)

    def trade_kv(n):
        def run(_, other, __):
            sib_tx[n] = other[n].astype(BF16)

        by_core(run)
        sib_copy(n).start()

    def reduce_kv(n):
        arrived(sib_rx.at[n], sib_rs.at[n])

        def run(own, _, raw):
            kv_tx[n] = (own[n] + sib_rx[n].astype(F32)).astype(BF16)
            by_member(lambda j: put(*kv_args(n, raw)[j]))

        by_core(run)

    def backward(i, n):
        p = prob[i, n]
        dp = dot(vb[n], gt[i])
        ds = (p.astype(F32) * (dp - rows[i, 0:1])).astype(BF16)
        dv_acc[n] += dot_nt(p, gft[i])
        dk_acc[n] += dot_nt(ds, qft[i])
        dqt[i] += dot(kt[n], ds)

    def send_dq(i):
        dq_tx[i] = (dqt[i] * rows[i, 1:2]).T.astype(BF16)
        put(*dq_args(i))

    def loop(lo, hi, body):
        def run(n, carry):
            body(n)
            return carry

        lax.fori_loop(lo, hi, run, 0)

    pending += cross(1)
    peaks = []
    for i in range(NB):
        m, mx = forward(i, mx)
        peaks.append(m)
        if i == 2:
            finish(0, peaks[0])
            finish(1, peaks[1])
    finish(2, peaks[2])
    finish(3, peaks[3])

    def early(i):
        def pair(n):
            backward(i, 2 * n)
            backward(i, 2 * n + 1)

        combine(i)
        loop(0, NB // 2, pair)
        send_dq(i)

    loop(0, 2, lambda t: early(1 + 2 * t))
    combine(2)
    combine(0)

    def both(t):
        n = 3 - 2 * t
        backward(2, n)
        backward(0, n)
        trade_kv(n)

    def relay_now():
        for arr in range(2):
            arrived(yr.at[arr], yr_rs.at[arr])
            relay_down(arr).start()

    passed = order(lax.rem(z - 2 * lax.rem(y + 1, 2) - c + 4, 4))

    loop(0, 2, both)
    reduce_kv(jnp.int32(3))
    backward(2, 2)
    backward(2, 0)
    send_dq(2)
    reduce_kv(jnp.int32(1))

    def final(t):
        pl.when(passed == 3 - 2 * t)(relay_now)
        n = 2 - 2 * t
        backward(0, n)
        trade_kv(n)

    loop(0, 2, final)
    reduce_kv(jnp.int32(2))
    send_dq(0)
    reduce_kv(jnp.int32(0))
    pl.when(lax.rem(passed, 2) == 0)(relay_now)

    for j in range(2):
        for n in range(2):
            arrived(dq_rx.at[j, n], dq_rs.at[j, n])
        for arr, raw in ((0, dk_rx), (1, dv_rx)):
            arrived(raw.at[:, cols(j)], kv_rs.at[arr, j])

    for copy in pending:
        copy.wait_send()
    for arr in range(2):
        for j in range(2):
            sent(*home_kv(arr, j))

    @pl.when(relay)
    def _():
        for arr in range(2):
            for n in range(NB):
                forward_kv(arr, n).wait_send()

    for i in range(NB):
        sent(*dq_args(jnp.int32(i)))
        sent(*kv_args(jnp.int32(i), dk_rx)[0])
        sib_copy(i).wait_send()
    for arr in range(2):
        relay_down(arr).wait_send()


def collect(dq_raw, dk_raw, dv_raw, dq_out, dk_out, dv_out):
    for j in range(2):
        total = dq_raw[j, 0].astype(F32) + dq_raw[j, 1].astype(F32)
        dq_out[:, j * HEAD_DIM : (j + 1) * HEAD_DIM] = total.astype(BF16)
    dk_out[...] = dk_raw[...]
    dv_out[...] = dv_raw[...]


def per_device(queries, key_states, value_states, out_grad):
    rows, width = queries.shape
    shape = jax.ShapeDtypeStruct((rows, width), BF16)
    vm = pltpu.VMEM
    dma = pltpu.SemaphoreType.DMA
    tile = (NB, BLK, HEAD_DIM)
    tile_t = (NB, HEAD_DIM, BLK)
    flops = 6 * 2 * (NB * BLK) ** 2 * HEAD_DIM
    raw = pl.pallas_call(
        kernel,
        out_shape=(jax.ShapeDtypeStruct((2, 2, BLK, HEAD_DIM), BF16), shape, shape),
        in_specs=[pl.BlockSpec(memory_space=pl.ANY)] * 4,
        out_specs=tuple([pl.BlockSpec(memory_space=pl.ANY)] * 3),
        scratch_shapes=[
            vm(tile, BF16), vm(tile, BF16), vm((2, 2, BLK, HEAD_DIM), BF16), vm((2,) + tile, BF16), vm((2, NB - 1, BLK, HEAD_DIM), BF16),
            vm(tile_t, BF16), vm((NB, AUG, BLK), BF16), vm(tile_t, BF16), vm(tile_t, BF16),
            vm(tile_t, BF16), vm(tile_t, BF16),
            vm((NB, BLK, BLK), F32), vm((NB, BLK, BLK), F32), vm((NB, NB, BLK, BLK), BF16), vm((NB, AUG, BLK), F32),
            vm((NB, 8, BLK), F32), vm((NB, 8, BLK), F32), vm((NB, 8, BLK), F32), vm(tile_t, F32),
            vm(tile, F32), vm(tile, F32),
            vm(tile, BF16), vm(tile, BF16), vm(tile, BF16), vm(tile, BF16), vm((2, BLK, HEAD_DIM), BF16),
            dma((NB,)), dma((NB,)), dma((2, 2)), dma((2, NB)), dma((2, NB - 1)), dma((NB,)), dma((NB,)), dma((2, 2)), dma((2, 2)), dma((2,)),
            dma((2, 2)), dma((2, 2)), dma((2, 2)), dma((2, NB)), dma((2, 3)), dma((NB,)), dma((NB,)), dma((NB,)), dma((NB,)), dma((2,)),
        ],
        compiler_params=pltpu.CompilerParams(
            collective_id=0, has_side_effects=True, vmem_limit_bytes=62 * 1024 * 1024
        ),
        cost_estimate=pl.CostEstimate(flops=flops, bytes_accessed=4 * rows * width * 2, transcendentals=(NB * BLK) ** 2),
    )(queries, key_states, value_states, out_grad)
    whole = pl.BlockSpec(memory_space=pltpu.VMEM)
    return pl.pallas_call(
        collect,
        out_shape=(shape, shape, shape),
        in_specs=[whole] * 3,
        out_specs=(whole,) * 3,
    )(*raw)


def solution(mesh):
    placed = (
        P("row", ("head", "col")),
        P("col", ("head", "row")),
        P("col", ("head", "row")),
        P("row", ("head", "col")),
    )
    return jax.shard_map(
        per_device,
        mesh=mesh,
        in_specs=placed,
        out_specs=(P("row", ("head", "col")), P("col", ("head", "row")), P("col", ("head", "row"))),
        check_vma=False,
    )
```

```python
import math

import jax
import jax.numpy as jnp
from jax import lax
from jax.experimental import pallas as pl
from jax.experimental.pallas import tpu as pltpu
from jax.sharding import PartitionSpec as P

HEAD_DIM = 128
BLK = 768
NB = 4
AUG = 144
SCALE = 1.0 / math.sqrt(HEAD_DIM)
LOG2E = math.log2(math.e)
MESH = pl.DeviceIdType.MESH
F32 = jnp.float32
BF16 = jnp.bfloat16


def order(d):
    return jnp.where(d == 2, 3, jnp.where(d == 3, 2, d))


def y_of(p, j):
    return lax.rem(p // 2 + j, 4)


def dot(a, b):
    return jnp.dot(a, b, preferred_element_type=F32)


def dot_nt(a, b):
    return lax.dot_general(a, b, (((1,), (1,)), ((), ())), preferred_element_type=F32)


def kernel(
    q_in, k_in, v_in, g_in,
    dq_rx, dk_rx, dv_rx,
    kb, vb, xr, via, qgb, kt, vt, qt, gt, qft, gft,
    s0, s1, prob, ot, stat_tx, stat_rx, rows, dqt, dk_acc, dv_acc,
    dq_tx, sib_tx, sib_rx, kv_tx, yr,
    k_rs, v_rs, xr_rs, via_rs, qg_rs, st_rs, sib_rs, dq_rs, kv_rs, yr_rs,
    home_ss, xr_ss, self_s, fwd_ss, hop_ss, st_ss, sib_ss, dq_ss, kv_ss, yr_ss,
):
    r, col, g = lax.axis_index("row"), lax.axis_index("col"), lax.axis_index("head")
    y, c = r // 2, lax.rem(r, 2)
    xh, z = col // 4, lax.rem(col, 4)
    jw = lax.rem(y + z // 2, 2)
    pw = z + 4 * (lax.rem(y - jw + 4, 4) // 2)
    aw = lax.rem(pw, 2)
    pk, pq = r, col
    partner = (y, c, 1 - xh, z)
    sibling = (y, 1 - c, xh, z)
    relay = c == aw

    up, down = lax.rem(xh + g, 2), lax.rem(xh + 1 - g, 2)

    def dev(t):
        yy, cc, xx, zz = t[:4]
        return (2 * yy + cc, 4 * xx + zz, g if len(t) == 4 else t[4])

    def is_me(t):
        yy, cc, xx, zz = t
        return jnp.logical_and(2 * yy + cc == r, 4 * xx + zz == col)

    barrier = pltpu.get_barrier_semaphore()
    greeted = [partner, sibling] + [(y, c, xx, z, 1 - g) for xx in (up, down)]
    greeted += [(lax.rem(y + d, 4), c, xh, z) for d in (1, 2, 3)]
    greeted += [(y_of(pk, j), cc, xh, lax.rem(pk, 4)) for j in range(2) for cc in range(2)]
    greeted += [(pw // 2, aw, xh, lax.rem(z + d, 4)) for d in range(4)]
    greeted += [(y, cc, xh, lax.rem(z + d, 4)) for d in (1, 2, 3) for cc in range(2)]
    greeted += [(lax.rem(y + d, 4), c, pw // 4, lax.rem(pw, 4)) for d in range(4)]
    greeted += [(y_of(pq, j), c, xx, z) for j in range(2) for xx in range(2)]
    for t in greeted:
        pl.semaphore_signal(barrier, inc=1, device_id=dev(t), device_id_type=MESH)
    pl.semaphore_wait(barrier, len(greeted))

    def remote(src, dst, t, ssem, rsem):
        return pltpu.make_async_remote_copy(
            src_ref=src, dst_ref=dst, send_sem=ssem, recv_sem=rsem, device_id=dev(t), device_id_type=MESH
        )

    def put(src, dst, t, ssem, rsem):
        me = is_me(t)

        @pl.when(jnp.logical_not(me))
        def _():
            remote(src, dst, t, ssem, rsem).start()

        @pl.when(me)
        def _():
            pltpu.make_async_copy(src, dst, rsem).start()

    def sent(src, dst, t, ssem, rsem):
        @pl.when(jnp.logical_not(is_me(t)))
        def _():
            remote(src, dst, t, ssem, rsem).wait_send()

    def arrived(dst, rsem):
        pltpu.make_async_copy(dst, dst, rsem).wait()

    def cols(j):
        return pl.ds(j * HEAD_DIM, HEAD_DIM)

    def spread(arr, ref):
        out = []
        for j, xx in enumerate((up, down)):
            slot = y_of(pq, j)
            pltpu.make_async_copy(ref.at[:, cols(j)], via.at[arr, slot], via_rs.at[arr, slot]).start()
            t = (y, c, xx, z, 1 - g)
            out.append(remote(ref.at[:, cols(j)], xr.at[arr, j], t, home_ss.at[arr, j], xr_rs.at[arr, j]))
            out[-1].start()
        return out

    def cross(arr):
        out = []
        for j, (origin, xx) in enumerate(((down, up), (up, down))):
            slot = y_of(4 * origin + z, j)
            arrived(xr.at[arr, j], xr_rs.at[arr, j])
            out.append(
                remote(xr.at[arr, j], via.at[arr, slot], (y, c, xx, z, 1 - g), xr_ss.at[arr, j], via_rs.at[arr, slot])
            )
            out[-1].start()
        return out

    def hop(arr):
        out = []
        for n, d in enumerate((1, 3, 2)):
            to = lax.rem(y + d, 4)
            slot = {3: 1, 1: 2, 2: 3}[d]
            arrived(via.at[arr, to], via_rs.at[arr, to])
            out.append(
                remote(via.at[arr, to], qgb.at[arr, slot - 1], (to, c, xh, z), hop_ss.at[arr, n], qg_rs.at[arr, slot - 1])
            )
            out[-1].start()
        return out

    def home_kv(arr, j):
        ref, buf, sem = ((k_in, kb, k_rs), (v_in, vb, v_rs))[arr]
        slot = order(lax.rem(z - lax.rem(pk, 4) + 4, 4))
        t = (y_of(pk, j), c, xh, lax.rem(pk, 4))
        return (ref.at[:, cols(j)], buf.at[slot], t, self_s.at[arr, j], sem.at[slot])

    def forward_kv(arr, n):
        buf, sem = ((kb, k_rs), (vb, v_rs))[arr]
        return remote(buf.at[n], buf.at[n], sibling, fwd_ss.at[arr, n], sem.at[n])

    pending = spread(0, q_in)
    for arr in range(2):
        for j in range(2):
            put(*home_kv(arr, j))
    pending += spread(1, g_in)
    pending += cross(0)
    arrived(via.at[0, y], via_rs.at[0, y])
    qt[0] = via[0, y].T
    pending += hop(0)

    sbuf = (s0, s1)

    def scores(i, n, buf, m):
        s = dot(kb[n], qt[i])
        sbuf[buf][n] = s
        return jnp.maximum(m, jnp.max(s.reshape(BLK // 8, 8, BLK), axis=0))

    lowest = jnp.full((8, BLK), -jnp.inf, F32)
    def first_scores(n, m):
        arrived(kb.at[n], k_rs.at[n])

        @pl.when(relay)
        def _():
            forward_kv(0, n).start()

        kt[n] = kb[n].T
        return scores(0, n, 0, m)

    mx = lax.fori_loop(0, NB, first_scores, lowest)

    def fetch_v(n, carry):
        arrived(vb.at[n], v_rs.at[n])

        @pl.when(relay)
        def _():
            forward_kv(1, n).start()

        vt[n, :HEAD_DIM, :] = vb[n].T
        vt[n, HEAD_DIM:, :] = jnp.ones((AUG - HEAD_DIM, BLK), BF16)
        return carry

    pending += cross(1)
    lax.fori_loop(0, NB, fetch_v, 0)
    pending += hop(1)

    def weigh(i, n, buf, m):
        p = jnp.exp2((sbuf[buf][n] - m) * (SCALE * LOG2E)).astype(BF16)
        prob[i, n] = p
        ot[i] += dot(vt[n], p)

    def stat_copy(i):
        return remote(stat_tx.at[i], stat_rx.at[i], partner, st_ss.at[i], st_rs.at[i])

    def finish(i, m):
        if i == 0:
            arrived(via.at[1, y], via_rs.at[1, y])
            gt[0] = via[1, y].T
        else:
            arrived(qgb.at[1, i - 1], qg_rs.at[1, i - 1])
            gt[i] = qgb[1, i - 1].T
        stat_tx[i, 0:1] = m
        stat_tx[i, 1:2] = ot[i, HEAD_DIM : HEAD_DIM + 1]
        stat_tx[i, 2:3] = jnp.sum(gt[i].astype(F32) * ot[i, :HEAD_DIM], axis=0, keepdims=True)
        stat_copy(i).start()

    def forward(i, mx):
        buf = i % 2
        more = i + 1 < NB
        if more:
            arrived(qgb.at[0, i], qg_rs.at[0, i])
            qt[i + 1] = qgb[0, i].T
        m = jnp.max(mx, axis=0, keepdims=True)
        ot[i] = jnp.zeros((AUG, BLK), F32)

        def step(n, mx2):
            if more:
                mx2 = scores(i + 1, n, 1 - buf, mx2)
            weigh(i, n, buf, m)
            return mx2

        return m, lax.fori_loop(0, NB, step, lowest)

    def combine(i):
        stat_copy(i).wait()
        m0, l0, d0 = stat_tx[i, 0:1], stat_tx[i, 1:2], stat_tx[i, 2:3]
        m1, l1, d1 = stat_rx[i, 0:1], stat_rx[i, 1:2], stat_rx[i, 2:3]
        m = jnp.maximum(m0, m1)
        e0 = jnp.exp2((m0 - m) * (SCALE * LOG2E))
        e1 = jnp.exp2((m1 - m) * (SCALE * LOG2E))
        inv = 1.0 / (l0 * e0 + l1 * e1)
        f = e0 * inv
        rows[i, 0:1] = (d0 * e0 + d1 * e1) * inv
        rows[i, 1:2] = f * SCALE
        gft[i] = (gt[i].astype(F32) * f).astype(BF16)
        qft[i] = (qt[i].astype(F32) * (f * SCALE)).astype(BF16)
        dqt[i] = jnp.zeros((HEAD_DIM, BLK), F32)

    dk_acc[...] = jnp.zeros_like(dk_acc)
    dv_acc[...] = jnp.zeros_like(dv_acc)

    def dq_args(i):
        t = (lax.rem(y + order(i), 4), c, pw // 4, lax.rem(pw, 4))
        return (dq_tx.at[i], dq_rx.at[jw, xh], t, dq_ss.at[i], dq_rs.at[jw, xh])

    def sib_copy(n):
        return remote(sib_tx.at[n], sib_rx.at[n], sibling, sib_ss.at[n], sib_rs.at[n])

    def kv_args(n, raw):
        t = (y, aw, xh, lax.rem(z + order(n), 4))
        return [
            (kv_tx.at[n], raw.at[:, cols(0)], t, kv_ss.at[n], kv_rs.at[c, 0]),
            (kv_tx.at[n], yr.at[c], t, kv_ss.at[n], yr_rs.at[c]),
        ]

    def relay_down(arr):
        raw = (dk_rx, dv_rx)[arr]
        t = (lax.rem(y + 3, 4), c, xh, z)
        return remote(yr.at[arr], raw.at[:, cols(1)], t, yr_ss.at[arr], kv_rs.at[arr, 1])

    def by_core(run):
        @pl.when(c == 0)
        def _():
            run(dk_acc, dv_acc, dk_rx)

        @pl.when(c == 1)
        def _():
            run(dv_acc, dk_acc, dv_rx)

    def by_member(run):
        for j in range(2):

            @pl.when(jw == j)
            def _():
                run(j)

    def trade_kv(n):
        def run(_, other, __):
            sib_tx[n] = other[n].astype(BF16)

        by_core(run)
        sib_copy(n).start()

    def reduce_kv(n):
        arrived(sib_rx.at[n], sib_rs.at[n])

        def run(own, _, raw):
            kv_tx[n] = (own[n] + sib_rx[n].astype(F32)).astype(BF16)
            by_member(lambda j: put(*kv_args(n, raw)[j]))

        by_core(run)

    def backward(i, n):
        p = prob[i, n]
        dp = dot(vb[n], gt[i])
        ds = (p.astype(F32) * (dp - rows[i, 0:1])).astype(BF16)
        dv_acc[n] += dot_nt(p, gft[i])
        dk_acc[n] += dot_nt(ds, qft[i])
        dqt[i] += dot(kt[n], ds)

    def send_dq(i):
        dq_tx[i] = (dqt[i] * rows[i, 1:2]).T.astype(BF16)
        put(*dq_args(i))

    def loop(lo, hi, body):
        def run(n, carry):
            body(n)
            return carry

        lax.fori_loop(lo, hi, run, 0)

    peaks = []
    for i in range(NB):
        m, mx = forward(i, mx)
        peaks.append(m)
        if i == 2:
            finish(0, peaks[0])
            finish(1, peaks[1])
    finish(2, peaks[2])
    finish(3, peaks[3])

    def early(i):
        def pair(n):
            backward(i, 2 * n)
            backward(i, 2 * n + 1)

        combine(i)
        loop(0, NB // 2, pair)
        send_dq(i)

    loop(0, 2, lambda t: early(1 + 2 * t))
    combine(2)
    combine(0)

    def both(t):
        n = 3 - 2 * t
        backward(2, n)
        backward(0, n)
        trade_kv(n)

    def relay_now():
        for arr in range(2):
            arrived(yr.at[arr], yr_rs.at[arr])
            relay_down(arr).start()

    passed = order(lax.rem(z - 2 * lax.rem(y + 1, 2) - c + 4, 4))

    loop(0, 2, both)
    reduce_kv(jnp.int32(3))
    backward(2, 2)
    backward(2, 0)
    send_dq(2)
    reduce_kv(jnp.int32(1))

    def final(t):
        pl.when(passed == 3 - 2 * t)(relay_now)
        n = 2 - 2 * t
        backward(0, n)
        trade_kv(n)

    loop(0, 2, final)
    reduce_kv(jnp.int32(2))
    send_dq(0)
    reduce_kv(jnp.int32(0))
    pl.when(lax.rem(passed, 2) == 0)(relay_now)

    for j in range(2):
        for n in range(2):
            arrived(dq_rx.at[j, n], dq_rs.at[j, n])
        for arr, raw in ((0, dk_rx), (1, dv_rx)):
            arrived(raw.at[:, cols(j)], kv_rs.at[arr, j])

    for copy in pending:
        copy.wait_send()
    for arr in range(2):
        for j in range(2):
            sent(*home_kv(arr, j))

    @pl.when(relay)
    def _():
        for arr in range(2):
            for n in range(NB):
                forward_kv(arr, n).wait_send()

    for i in range(NB):
        sent(*dq_args(jnp.int32(i)))
        sent(*kv_args(jnp.int32(i), dk_rx)[0])
        sib_copy(i).wait_send()
    for arr in range(2):
        relay_down(arr).wait_send()


def collect(dq_raw, dk_raw, dv_raw, dq_out, dk_out, dv_out):
    for j in range(2):
        total = dq_raw[j, 0].astype(F32) + dq_raw[j, 1].astype(F32)
        dq_out[:, j * HEAD_DIM : (j + 1) * HEAD_DIM] = total.astype(BF16)
    dk_out[...] = dk_raw[...]
    dv_out[...] = dv_raw[...]


def per_device(queries, key_states, value_states, out_grad):
    rows, width = queries.shape
    shape = jax.ShapeDtypeStruct((rows, width), BF16)
    vm = pltpu.VMEM
    dma = pltpu.SemaphoreType.DMA
    tile = (NB, BLK, HEAD_DIM)
    tile_t = (NB, HEAD_DIM, BLK)
    flops = 6 * 2 * (NB * BLK) ** 2 * HEAD_DIM
    raw = pl.pallas_call(
        kernel,
        out_shape=(jax.ShapeDtypeStruct((2, 2, BLK, HEAD_DIM), BF16), shape, shape),
        in_specs=[pl.BlockSpec(memory_space=pl.ANY)] * 4,
        out_specs=tuple([pl.BlockSpec(memory_space=pl.ANY)] * 3),
        scratch_shapes=[
            vm(tile, BF16), vm(tile, BF16), vm((2, 2, BLK, HEAD_DIM), BF16), vm((2,) + tile, BF16), vm((2, NB - 1, BLK, HEAD_DIM), BF16),
            vm(tile_t, BF16), vm((NB, AUG, BLK), BF16), vm(tile_t, BF16), vm(tile_t, BF16),
            vm(tile_t, BF16), vm(tile_t, BF16),
            vm((NB, BLK, BLK), F32), vm((NB, BLK, BLK), F32), vm((NB, NB, BLK, BLK), BF16), vm((NB, AUG, BLK), F32),
            vm((NB, 8, BLK), F32), vm((NB, 8, BLK), F32), vm((NB, 8, BLK), F32), vm(tile_t, F32),
            vm(tile, F32), vm(tile, F32),
            vm(tile, BF16), vm(tile, BF16), vm(tile, BF16), vm(tile, BF16), vm((2, BLK, HEAD_DIM), BF16),
            dma((NB,)), dma((NB,)), dma((2, 2)), dma((2, NB)), dma((2, NB - 1)), dma((NB,)), dma((NB,)), dma((2, 2)), dma((2, 2)), dma((2,)),
            dma((2, 2)), dma((2, 2)), dma((2, 2)), dma((2, NB)), dma((2, 3)), dma((NB,)), dma((NB,)), dma((NB,)), dma((NB,)), dma((2,)),
        ],
        compiler_params=pltpu.CompilerParams(
            collective_id=0, has_side_effects=True, vmem_limit_bytes=62 * 1024 * 1024
        ),
        cost_estimate=pl.CostEstimate(flops=flops, bytes_accessed=4 * rows * width * 2, transcendentals=(NB * BLK) ** 2),
    )(queries, key_states, value_states, out_grad)
    whole = pl.BlockSpec(memory_space=pltpu.VMEM)
    return pl.pallas_call(
        collect,
        out_shape=(shape, shape, shape),
        in_specs=[whole] * 3,
        out_specs=(whole,) * 3,
    )(*raw)


def solution(mesh):
    placed = (
        P("row", ("head", "col")),
        P("col", ("head", "row")),
        P("col", ("head", "row")),
        P("row", ("head", "col")),
    )
    return jax.shard_map(
        per_device,
        mesh=mesh,
        in_specs=placed,
        out_specs=(P("row", ("head", "col")), P("col", ("head", "row")), P("col", ("head", "row"))),
        check_vma=False,
    )
```

```python
import math

import jax
import jax.numpy as jnp
from jax import lax
from jax.experimental import pallas as pl
from jax.experimental.pallas import tpu as pltpu
from jax.sharding import PartitionSpec as P

HEAD_DIM = 128
BLK = 768
NB = 4
AUG = 144
SCALE = 1.0 / math.sqrt(HEAD_DIM)
LOG2E = math.log2(math.e)
MESH = pl.DeviceIdType.MESH
F32 = jnp.float32
BF16 = jnp.bfloat16


def order(d):
    return jnp.where(d == 2, 3, jnp.where(d == 3, 2, d))


def y_of(p, j):
    return lax.rem(p // 2 + j, 4)


def dot(a, b):
    return jnp.dot(a, b, preferred_element_type=F32)


def dot_nt(a, b):
    return lax.dot_general(a, b, (((1,), (1,)), ((), ())), preferred_element_type=F32)


def kernel(
    q_in, k_in, v_in, g_in,
    dq_rx, dk_rx, dv_rx,
    kb, vb, xr, via, qgb, kt, vt, qt, gt, qft, gft,
    s0, s1, prob, ot, stat_tx, stat_rx, rows, dqt, dk_acc, dv_acc,
    dq_tx, sib_tx, sib_rx, kv_tx, yr,
    k_rs, v_rs, xr_rs, via_rs, qg_rs, st_rs, sib_rs, dq_rs, kv_rs, yr_rs,
    home_ss, xr_ss, self_s, fwd_ss, hop_ss, st_ss, sib_ss, dq_ss, kv_ss, yr_ss,
):
    r, col, g = lax.axis_index("row"), lax.axis_index("col"), lax.axis_index("head")
    y, c = r // 2, lax.rem(r, 2)
    xh, z = col // 4, lax.rem(col, 4)
    jw = lax.rem(y + z // 2, 2)
    pw = z + 4 * (lax.rem(y - jw + 4, 4) // 2)
    aw = lax.rem(pw, 2)
    pk, pq = r, col
    partner = (y, c, 1 - xh, z)
    sibling = (y, 1 - c, xh, z)
    relay = c == aw

    up, down = lax.rem(xh + g, 2), lax.rem(xh + 1 - g, 2)

    def dev(t):
        yy, cc, xx, zz = t[:4]
        return (2 * yy + cc, 4 * xx + zz, g if len(t) == 4 else t[4])

    def is_me(t):
        yy, cc, xx, zz = t
        return jnp.logical_and(2 * yy + cc == r, 4 * xx + zz == col)

    barrier = pltpu.get_barrier_semaphore()
    greeted = [partner, sibling] + [(y, c, xx, z, 1 - g) for xx in (up, down)]
    greeted += [(lax.rem(y + d, 4), c, xh, z) for d in (1, 2, 3)]
    greeted += [(y_of(pk, j), cc, xh, lax.rem(pk, 4)) for j in range(2) for cc in range(2)]
    greeted += [(pw // 2, aw, xh, lax.rem(z + d, 4)) for d in range(4)]
    greeted += [(y, cc, xh, lax.rem(z + d, 4)) for d in (1, 2, 3) for cc in range(2)]
    greeted += [(lax.rem(y + d, 4), c, pw // 4, lax.rem(pw, 4)) for d in range(4)]
    greeted += [(y_of(pq, j), c, xx, z) for j in range(2) for xx in range(2)]
    for t in greeted:
        pl.semaphore_signal(barrier, inc=1, device_id=dev(t), device_id_type=MESH)
    pl.semaphore_wait(barrier, len(greeted))

    def remote(src, dst, t, ssem, rsem):
        return pltpu.make_async_remote_copy(
            src_ref=src, dst_ref=dst, send_sem=ssem, recv_sem=rsem, device_id=dev(t), device_id_type=MESH
        )

    def put(src, dst, t, ssem, rsem):
        me = is_me(t)

        @pl.when(jnp.logical_not(me))
        def _():
            remote(src, dst, t, ssem, rsem).start()

        @pl.when(me)
        def _():
            pltpu.make_async_copy(src, dst, rsem).start()

    def sent(src, dst, t, ssem, rsem):
        @pl.when(jnp.logical_not(is_me(t)))
        def _():
            remote(src, dst, t, ssem, rsem).wait_send()

    def arrived(dst, rsem):
        pltpu.make_async_copy(dst, dst, rsem).wait()

    def cols(j):
        return pl.ds(j * HEAD_DIM, HEAD_DIM)

    def spread(arr, ref):
        out = []
        for j, xx in enumerate((up, down)):
            slot = y_of(pq, j)
            pltpu.make_async_copy(ref.at[:, cols(j)], via.at[arr, slot], via_rs.at[arr, slot]).start()
            t = (y, c, xx, z, 1 - g)
            out.append(remote(ref.at[:, cols(j)], xr.at[arr, j], t, home_ss.at[arr, j], xr_rs.at[arr, j]))
            out[-1].start()
        return out

    def cross(arr):
        out = []
        for j, (origin, xx) in enumerate(((down, up), (up, down))):
            slot = y_of(4 * origin + z, j)
            arrived(xr.at[arr, j], xr_rs.at[arr, j])
            out.append(
                remote(xr.at[arr, j], via.at[arr, slot], (y, c, xx, z, 1 - g), xr_ss.at[arr, j], via_rs.at[arr, slot])
            )
            out[-1].start()
        return out

    def hop(arr):
        out = []
        for n, d in enumerate((1, 3, 2)):
            to = lax.rem(y + d, 4)
            slot = {3: 1, 1: 2, 2: 3}[d]
            arrived(via.at[arr, to], via_rs.at[arr, to])
            out.append(
                remote(via.at[arr, to], qgb.at[arr, slot - 1], (to, c, xh, z), hop_ss.at[arr, n], qg_rs.at[arr, slot - 1])
            )
            out[-1].start()
        return out

    def home_kv(arr, j):
        ref, buf, sem = ((k_in, kb, k_rs), (v_in, vb, v_rs))[arr]
        slot = order(lax.rem(z - lax.rem(pk, 4) + 4, 4))
        t = (y_of(pk, j), c, xh, lax.rem(pk, 4))
        return (ref.at[:, cols(j)], buf.at[slot], t, self_s.at[arr, j], sem.at[slot])

    def forward_kv(arr, n):
        buf, sem = ((kb, k_rs), (vb, v_rs))[arr]
        return remote(buf.at[n], buf.at[n], sibling, fwd_ss.at[arr, n], sem.at[n])

    pending = spread(0, q_in)
    for arr in range(2):
        for j in range(2):
            put(*home_kv(arr, j))
    pending += spread(1, g_in)
    for total in (dk_acc, dv_acc, dqt, ot):
        total[...] = jnp.zeros_like(total)
    pending += cross(0)
    arrived(via.at[0, y], via_rs.at[0, y])
    qt[0] = via[0, y].T
    pending += hop(0)

    sbuf = (s0, s1)

    def scores(i, n, buf, m):
        s = dot(kb[n], qt[i])
        sbuf[buf][n] = s
        return jnp.maximum(m, jnp.max(s.reshape(BLK // 8, 8, BLK), axis=0))

    lowest = jnp.full((8, BLK), -jnp.inf, F32)
    def first_scores(n, m):
        arrived(kb.at[n], k_rs.at[n])

        @pl.when(relay)
        def _():
            forward_kv(0, n).start()

        kt[n] = kb[n].T
        return scores(0, n, 0, m)

    mx = lax.fori_loop(0, NB, first_scores, lowest)

    def fetch_v(n, carry):
        arrived(vb.at[n], v_rs.at[n])

        @pl.when(relay)
        def _():
            forward_kv(1, n).start()

        vt[n, :HEAD_DIM, :] = vb[n].T
        vt[n, HEAD_DIM:, :] = jnp.ones((AUG - HEAD_DIM, BLK), BF16)
        return carry

    lax.fori_loop(0, NB, fetch_v, 0)
    pending += cross(1)

    def weigh(i, n, buf, m):
        p = jnp.exp2((sbuf[buf][n] - m) * (SCALE * LOG2E)).astype(BF16)
        prob[i, n] = p
        ot[i] += dot(vt[n], p)

    def stat_copy(i):
        return remote(stat_tx.at[i], stat_rx.at[i], partner, st_ss.at[i], st_rs.at[i])

    def finish(i, m):
        if i == 0:
            arrived(via.at[1, y], via_rs.at[1, y])
            gt[0] = via[1, y].T
        else:
            arrived(qgb.at[1, i - 1], qg_rs.at[1, i - 1])
            gt[i] = qgb[1, i - 1].T
        stat_tx[i, 0:1] = m
        stat_tx[i, 1:2] = ot[i, HEAD_DIM : HEAD_DIM + 1]
        stat_tx[i, 2:3] = jnp.sum(gt[i].astype(F32) * ot[i, :HEAD_DIM], axis=0, keepdims=True)
        stat_copy(i).start()

    def forward(i, mx):
        buf = i % 2
        more = i + 1 < NB
        if more:
            arrived(qgb.at[0, i], qg_rs.at[0, i])
            qt[i + 1] = qgb[0, i].T
        m = jnp.max(mx, axis=0, keepdims=True)

        def step(at, mx2):
            for n in (2 * at, 2 * at + 1):
                if more:
                    mx2 = scores(i + 1, n, 1 - buf, mx2)
                weigh(i, n, buf, m)
            return mx2

        return m, lax.fori_loop(0, NB // 2, step, lowest)

    def combine(i):
        stat_copy(i).wait()
        m0, l0, d0 = stat_tx[i, 0:1], stat_tx[i, 1:2], stat_tx[i, 2:3]
        m1, l1, d1 = stat_rx[i, 0:1], stat_rx[i, 1:2], stat_rx[i, 2:3]
        m = jnp.maximum(m0, m1)
        e0 = jnp.exp2((m0 - m) * (SCALE * LOG2E))
        e1 = jnp.exp2((m1 - m) * (SCALE * LOG2E))
        inv = 1.0 / (l0 * e0 + l1 * e1)
        f = e0 * inv
        rows[i, 0:1] = (d0 * e0 + d1 * e1) * inv
        rows[i, 1:2] = f * SCALE
        gft[i] = (gt[i].astype(F32) * f).astype(BF16)
        qft[i] = (qt[i].astype(F32) * (f * SCALE)).astype(BF16)


    def dq_args(i):
        t = (lax.rem(y + order(i), 4), c, pw // 4, lax.rem(pw, 4))
        return (dq_tx.at[i], dq_rx.at[jw, xh], t, dq_ss.at[i], dq_rs.at[jw, xh])

    def sib_copy(n):
        return remote(sib_tx.at[n], sib_rx.at[n], sibling, sib_ss.at[n], sib_rs.at[n])

    def kv_args(n, raw):
        t = (y, aw, xh, lax.rem(z + order(n), 4))
        return [
            (kv_tx.at[n], raw.at[:, cols(0)], t, kv_ss.at[n], kv_rs.at[c, 0]),
            (kv_tx.at[n], yr.at[c], t, kv_ss.at[n], yr_rs.at[c]),
        ]

    def relay_down(arr):
        raw = (dk_rx, dv_rx)[arr]
        t = (lax.rem(y + 3, 4), c, xh, z)
        return remote(yr.at[arr], raw.at[:, cols(1)], t, yr_ss.at[arr], kv_rs.at[arr, 1])

    def by_core(run):
        @pl.when(c == 0)
        def _():
            run(dk_acc, dv_acc, dk_rx)

        @pl.when(c == 1)
        def _():
            run(dv_acc, dk_acc, dv_rx)

    def by_member(run):
        for j in range(2):

            @pl.when(jw == j)
            def _():
                run(j)

    def trade_kv(n):
        def run(_, other, __):
            sib_tx[n] = other[n].astype(BF16)

        by_core(run)
        sib_copy(n).start()

    def reduce_kv(n):
        arrived(sib_rx.at[n], sib_rs.at[n])

        def run(own, _, raw):
            kv_tx[n] = (own[n] + sib_rx[n].astype(F32)).astype(BF16)
            by_member(lambda j: put(*kv_args(n, raw)[j]))

        by_core(run)

    def backward(i, n):
        p = prob[i, n]
        dp = dot(vb[n], gt[i])
        ds = (p.astype(F32) * (dp - rows[i, 0:1])).astype(BF16)
        dv_acc[n] += dot_nt(p, gft[i])
        dk_acc[n] += dot_nt(ds, qft[i])
        dqt[i] += dot(kt[n], ds)

    def send_dq(i):
        dq_tx[i] = (dqt[i] * rows[i, 1:2]).T.astype(BF16)
        put(*dq_args(i))

    def loop(lo, hi, body):
        def run(n, carry):
            body(n)
            return carry

        lax.fori_loop(lo, hi, run, 0)

    peaks = []
    for i in range(NB):
        m, mx = forward(i, mx)
        peaks.append(m)
        if i == 0:
            pending += hop(1)
        if i == 2:
            finish(0, peaks[0])
            finish(1, peaks[1])
    finish(2, peaks[2])
    finish(3, peaks[3])

    def early(i):
        def pair(n):
            backward(i, 2 * n)
            backward(i, 2 * n + 1)

        combine(i)
        loop(0, NB // 2, pair)
        send_dq(i)

    loop(0, 2, lambda t: early(1 + 2 * t))
    combine(2)
    combine(0)

    def both(t):
        n = 3 - 2 * t
        backward(2, n)
        backward(0, n)
        trade_kv(n)

    def relay_now():
        for arr in range(2):
            arrived(yr.at[arr], yr_rs.at[arr])
            relay_down(arr).start()

    passed = order(lax.rem(z - 2 * lax.rem(y + 1, 2) - c + 4, 4))

    loop(0, 2, both)
    reduce_kv(jnp.int32(3))
    backward(2, 2)
    backward(2, 0)
    send_dq(2)
    reduce_kv(jnp.int32(1))

    def final(t):
        pl.when(passed == 3 - 2 * t)(relay_now)
        n = 2 - 2 * t
        backward(0, n)
        trade_kv(n)

    loop(0, 2, final)
    reduce_kv(jnp.int32(2))
    send_dq(0)
    reduce_kv(jnp.int32(0))
    pl.when(lax.rem(passed, 2) == 0)(relay_now)

    for j in range(2):
        for n in range(2):
            arrived(dq_rx.at[j, n], dq_rs.at[j, n])
        for arr, raw in ((0, dk_rx), (1, dv_rx)):
            arrived(raw.at[:, cols(j)], kv_rs.at[arr, j])

    for copy in pending:
        copy.wait_send()
    for arr in range(2):
        for j in range(2):
            sent(*home_kv(arr, j))

    @pl.when(relay)
    def _():
        for arr in range(2):
            for n in range(NB):
                forward_kv(arr, n).wait_send()

    for i in range(NB):
        sent(*dq_args(jnp.int32(i)))
        sent(*kv_args(jnp.int32(i), dk_rx)[0])
        sib_copy(i).wait_send()
    for arr in range(2):
        relay_down(arr).wait_send()


def collect(dq_raw, dk_raw, dv_raw, dq_out, dk_out, dv_out):
    for j in range(2):
        total = dq_raw[j, 0].astype(F32) + dq_raw[j, 1].astype(F32)
        dq_out[:, j * HEAD_DIM : (j + 1) * HEAD_DIM] = total.astype(BF16)
    dk_out[...] = dk_raw[...]
    dv_out[...] = dv_raw[...]


def per_device(queries, key_states, value_states, out_grad):
    rows, width = queries.shape
    shape = jax.ShapeDtypeStruct((rows, width), BF16)
    vm = pltpu.VMEM
    dma = pltpu.SemaphoreType.DMA
    tile = (NB, BLK, HEAD_DIM)
    tile_t = (NB, HEAD_DIM, BLK)
    flops = 6 * 2 * (NB * BLK) ** 2 * HEAD_DIM
    raw = pl.pallas_call(
        kernel,
        out_shape=(jax.ShapeDtypeStruct((2, 2, BLK, HEAD_DIM), BF16), shape, shape),
        in_specs=[pl.BlockSpec(memory_space=pl.ANY)] * 4,
        out_specs=tuple([pl.BlockSpec(memory_space=pl.ANY)] * 3),
        scratch_shapes=[
            vm(tile, BF16), vm(tile, BF16), vm((2, 2, BLK, HEAD_DIM), BF16), vm((2,) + tile, BF16), vm((2, NB - 1, BLK, HEAD_DIM), BF16),
            vm(tile_t, BF16), vm((NB, AUG, BLK), BF16), vm(tile_t, BF16), vm(tile_t, BF16),
            vm(tile_t, BF16), vm(tile_t, BF16),
            vm((NB, BLK, BLK), F32), vm((NB, BLK, BLK), F32), vm((NB, NB, BLK, BLK), BF16), vm((NB, AUG, BLK), F32),
            vm((NB, 8, BLK), F32), vm((NB, 8, BLK), F32), vm((NB, 8, BLK), F32), vm(tile_t, F32),
            vm(tile, F32), vm(tile, F32),
            vm(tile, BF16), vm(tile, BF16), vm(tile, BF16), vm(tile, BF16), vm((2, BLK, HEAD_DIM), BF16),
            dma((NB,)), dma((NB,)), dma((2, 2)), dma((2, NB)), dma((2, NB - 1)), dma((NB,)), dma((NB,)), dma((2, 2)), dma((2, 2)), dma((2,)),
            dma((2, 2)), dma((2, 2)), dma((2, 2)), dma((2, NB)), dma((2, 3)), dma((NB,)), dma((NB,)), dma((NB,)), dma((NB,)), dma((2,)),
        ],
        compiler_params=pltpu.CompilerParams(
            collective_id=0, has_side_effects=True, vmem_limit_bytes=62 * 1024 * 1024
        ),
        cost_estimate=pl.CostEstimate(flops=flops, bytes_accessed=4 * rows * width * 2, transcendentals=(NB * BLK) ** 2),
    )(queries, key_states, value_states, out_grad)
    whole = pl.BlockSpec(memory_space=pltpu.VMEM)
    return pl.pallas_call(
        collect,
        out_shape=(shape, shape, shape),
        in_specs=[whole] * 3,
        out_specs=(whole,) * 3,
    )(*raw)


def solution(mesh):
    placed = (
        P("row", ("head", "col")),
        P("col", ("head", "row")),
        P("col", ("head", "row")),
        P("row", ("head", "col")),
    )
    return jax.shard_map(
        per_device,
        mesh=mesh,
        in_specs=placed,
        out_specs=(P("row", ("head", "col")), P("col", ("head", "row")), P("col", ("head", "row"))),
        check_vma=False,
    )
```

```python
import math

import jax
import jax.numpy as jnp
from jax import lax
from jax.experimental import pallas as pl
from jax.experimental.pallas import tpu as pltpu
from jax.sharding import PartitionSpec as P

HEAD_DIM = 128
BLK = 768
NB = 4
AUG = 144
SCALE = 1.0 / math.sqrt(HEAD_DIM)
LOG2E = math.log2(math.e)
MESH = pl.DeviceIdType.MESH
F32 = jnp.float32
BF16 = jnp.bfloat16


def order(d):
    return jnp.where(d == 2, 3, jnp.where(d == 3, 2, d))


def y_of(p, j):
    return lax.rem(p // 2 + j, 4)


def dot(a, b):
    return jnp.dot(a, b, preferred_element_type=F32)


def dot_nt(a, b):
    return lax.dot_general(a, b, (((1,), (1,)), ((), ())), preferred_element_type=F32)


def kernel(
    q_in, k_in, v_in, g_in,
    dq_rx, dk_rx, dv_rx,
    kb, vb, xr, via, qgb, kt, vt, qt, gt, qft, gft,
    s0, s1, prob, ot, stat_tx, stat_rx, rows, dqt, dk_acc, dv_acc,
    dq_tx, sib_tx, sib_rx, kv_tx, yr,
    k_rs, v_rs, xr_rs, via_rs, qg_rs, st_rs, sib_rs, dq_rs, kv_rs, yr_rs,
    home_ss, xr_ss, self_s, fwd_ss, hop_ss, st_ss, sib_ss, dq_ss, kv_ss, yr_ss,
):
    r, col, g = lax.axis_index("row"), lax.axis_index("col"), lax.axis_index("head")
    y, c = r // 2, lax.rem(r, 2)
    xh, z = col // 4, lax.rem(col, 4)
    jw = lax.rem(y + z // 2, 2)
    pw = z + 4 * (lax.rem(y - jw + 4, 4) // 2)
    aw = lax.rem(pw, 2)
    pk, pq = r, col
    partner = (y, c, 1 - xh, z)
    sibling = (y, 1 - c, xh, z)
    relay = c == aw

    up, down = lax.rem(xh + g, 2), lax.rem(xh + 1 - g, 2)

    def dev(t):
        yy, cc, xx, zz = t[:4]
        return (2 * yy + cc, 4 * xx + zz, g if len(t) == 4 else t[4])

    def is_me(t):
        yy, cc, xx, zz = t
        return jnp.logical_and(2 * yy + cc == r, 4 * xx + zz == col)

    barrier = pltpu.get_barrier_semaphore()
    greeted = [partner, sibling] + [(y, c, xx, z, 1 - g) for xx in (up, down)]
    greeted += [(lax.rem(y + d, 4), c, xh, z) for d in (1, 2, 3)]
    greeted += [(y_of(pk, j), cc, xh, lax.rem(pk, 4)) for j in range(2) for cc in range(2)]
    greeted += [(pw // 2, aw, xh, lax.rem(z + d, 4)) for d in range(4)]
    greeted += [(y, cc, xh, lax.rem(z + d, 4)) for d in (1, 2, 3) for cc in range(2)]
    greeted += [(lax.rem(y + d, 4), c, pw // 4, lax.rem(pw, 4)) for d in range(4)]
    greeted += [(y_of(pq, j), c, xx, z) for j in range(2) for xx in range(2)]
    for t in greeted:
        pl.semaphore_signal(barrier, inc=1, device_id=dev(t), device_id_type=MESH)
    pl.semaphore_wait(barrier, len(greeted))

    def remote(src, dst, t, ssem, rsem):
        return pltpu.make_async_remote_copy(
            src_ref=src, dst_ref=dst, send_sem=ssem, recv_sem=rsem, device_id=dev(t), device_id_type=MESH
        )

    def put(src, dst, t, ssem, rsem):
        me = is_me(t)

        @pl.when(jnp.logical_not(me))
        def _():
            remote(src, dst, t, ssem, rsem).start()

        @pl.when(me)
        def _():
            pltpu.make_async_copy(src, dst, rsem).start()

    def sent(src, dst, t, ssem, rsem):
        @pl.when(jnp.logical_not(is_me(t)))
        def _():
            remote(src, dst, t, ssem, rsem).wait_send()

    def arrived(dst, rsem):
        pltpu.make_async_copy(dst, dst, rsem).wait()

    def cols(j):
        return pl.ds(j * HEAD_DIM, HEAD_DIM)

    def spread(arr, ref):
        out = []
        for j, xx in enumerate((up, down)):
            slot = y_of(pq, j)
            pltpu.make_async_copy(ref.at[:, cols(j)], via.at[arr, slot], via_rs.at[arr, slot]).start()
            t = (y, c, xx, z, 1 - g)
            out.append(remote(ref.at[:, cols(j)], xr.at[arr, j], t, home_ss.at[arr, j], xr_rs.at[arr, j]))
            out[-1].start()
        return out

    def cross(arr):
        out = []
        for j, (origin, xx) in enumerate(((down, up), (up, down))):
            slot = y_of(4 * origin + z, j)
            arrived(xr.at[arr, j], xr_rs.at[arr, j])
            out.append(
                remote(xr.at[arr, j], via.at[arr, slot], (y, c, xx, z, 1 - g), xr_ss.at[arr, j], via_rs.at[arr, slot])
            )
            out[-1].start()
        return out

    def hop(arr):
        out = []
        for n, d in enumerate((1, 3, 2)):
            to = lax.rem(y + d, 4)
            slot = {3: 1, 1: 2, 2: 3}[d]
            arrived(via.at[arr, to], via_rs.at[arr, to])
            out.append(
                remote(via.at[arr, to], qgb.at[arr, slot - 1], (to, c, xh, z), hop_ss.at[arr, n], qg_rs.at[arr, slot - 1])
            )
            out[-1].start()
        return out

    def home_kv(arr, j):
        ref, buf, sem = ((k_in, kb, k_rs), (v_in, vb, v_rs))[arr]
        slot = order(lax.rem(z - lax.rem(pk, 4) + 4, 4))
        t = (y_of(pk, j), c, xh, lax.rem(pk, 4))
        return (ref.at[:, cols(j)], buf.at[slot], t, self_s.at[arr, j], sem.at[slot])

    def forward_kv(arr, n):
        buf, sem = ((kb, k_rs), (vb, v_rs))[arr]
        return remote(buf.at[n], buf.at[n], sibling, fwd_ss.at[arr, n], sem.at[n])

    pending = spread(0, q_in)
    for arr in range(2):
        for j in range(2):
            put(*home_kv(arr, j))
    pending += spread(1, g_in)
    for total in (dk_acc, dv_acc, dqt, ot):
        total[...] = jnp.zeros_like(total)
    pending += cross(0)

    def fetch_k(n, carry):
        arrived(kb.at[n], k_rs.at[n])

        @pl.when(relay)
        def _():
            forward_kv(0, n).start()

        return carry

    lax.fori_loop(0, NB, fetch_k, 0)
    arrived(via.at[0, y], via_rs.at[0, y])
    qt[0] = via[0, y].T
    pending += hop(0)

    sbuf = (s0, s1)

    def scores(i, n, buf, m):
        s = dot(kb[n], qt[i])
        sbuf[buf][n] = s
        return jnp.maximum(m, jnp.max(s.reshape(BLK // 8, 8, BLK), axis=0))

    lowest = jnp.full((8, BLK), -jnp.inf, F32)
    def first_scores(n, m):
        kt[n] = kb[n].T
        return scores(0, n, 0, m)

    mx = lax.fori_loop(0, NB, first_scores, lowest)

    def fetch_v(n, carry):
        arrived(vb.at[n], v_rs.at[n])

        @pl.when(relay)
        def _():
            forward_kv(1, n).start()

        vt[n, :HEAD_DIM, :] = vb[n].T
        vt[n, HEAD_DIM:, :] = jnp.ones((AUG - HEAD_DIM, BLK), BF16)
        return carry

    lax.fori_loop(0, NB, fetch_v, 0)
    pending += cross(1)

    def weigh(i, n, buf, m):
        p = jnp.exp2((sbuf[buf][n] - m) * (SCALE * LOG2E)).astype(BF16)
        prob[i, n] = p
        ot[i] += dot(vt[n], p)

    def stat_copy(i):
        return remote(stat_tx.at[i], stat_rx.at[i], partner, st_ss.at[i], st_rs.at[i])

    def finish(i, m):
        if i == 0:
            arrived(via.at[1, y], via_rs.at[1, y])
            gt[0] = via[1, y].T
        else:
            arrived(qgb.at[1, i - 1], qg_rs.at[1, i - 1])
            gt[i] = qgb[1, i - 1].T
        stat_tx[i, 0:1] = m
        stat_tx[i, 1:2] = ot[i, HEAD_DIM : HEAD_DIM + 1]
        stat_tx[i, 2:3] = jnp.sum(gt[i].astype(F32) * ot[i, :HEAD_DIM], axis=0, keepdims=True)
        stat_copy(i).start()

    def forward(i, mx):
        buf = i % 2
        more = i + 1 < NB
        if more:
            arrived(qgb.at[0, i], qg_rs.at[0, i])
            qt[i + 1] = qgb[0, i].T
        m = jnp.max(mx, axis=0, keepdims=True)

        def step(n, mx2):
            if more:
                mx2 = scores(i + 1, n, 1 - buf, mx2)
            weigh(i, n, buf, m)
            return mx2

        return m, lax.fori_loop(0, NB, step, lowest)

    def combine(i):
        stat_copy(i).wait()
        m0, l0, d0 = stat_tx[i, 0:1], stat_tx[i, 1:2], stat_tx[i, 2:3]
        m1, l1, d1 = stat_rx[i, 0:1], stat_rx[i, 1:2], stat_rx[i, 2:3]
        m = jnp.maximum(m0, m1)
        e0 = jnp.exp2((m0 - m) * (SCALE * LOG2E))
        e1 = jnp.exp2((m1 - m) * (SCALE * LOG2E))
        inv = 1.0 / (l0 * e0 + l1 * e1)
        f = e0 * inv
        rows[i, 0:1] = (d0 * e0 + d1 * e1) * inv
        rows[i, 1:2] = f * SCALE
        gft[i] = (gt[i].astype(F32) * f).astype(BF16)
        qft[i] = (qt[i].astype(F32) * (f * SCALE)).astype(BF16)


    def dq_args(i):
        t = (lax.rem(y + order(i), 4), c, pw // 4, lax.rem(pw, 4))
        return (dq_tx.at[i], dq_rx.at[jw, xh], t, dq_ss.at[i], dq_rs.at[jw, xh])

    def sib_copy(n):
        return remote(sib_tx.at[n], sib_rx.at[n], sibling, sib_ss.at[n], sib_rs.at[n])

    def kv_args(n, raw):
        t = (y, aw, xh, lax.rem(z + order(n), 4))
        return [
            (kv_tx.at[n], raw.at[:, cols(0)], t, kv_ss.at[n], kv_rs.at[c, 0]),
            (kv_tx.at[n], yr.at[c], t, kv_ss.at[n], yr_rs.at[c]),
        ]

    def relay_down(arr):
        raw = (dk_rx, dv_rx)[arr]
        t = (lax.rem(y + 3, 4), c, xh, z)
        return remote(yr.at[arr], raw.at[:, cols(1)], t, yr_ss.at[arr], kv_rs.at[arr, 1])

    def by_core(run):
        @pl.when(c == 0)
        def _():
            run(dk_acc, dv_acc, dk_rx)

        @pl.when(c == 1)
        def _():
            run(dv_acc, dk_acc, dv_rx)

    def by_member(run):
        for j in range(2):

            @pl.when(jw == j)
            def _():
                run(j)

    def trade_kv(n):
        def run(_, other, __):
            sib_tx[n] = other[n].astype(BF16)

        by_core(run)
        sib_copy(n).start()

    def reduce_kv(n):
        arrived(sib_rx.at[n], sib_rs.at[n])

        def run(own, _, raw):
            kv_tx[n] = (own[n] + sib_rx[n].astype(F32)).astype(BF16)
            by_member(lambda j: put(*kv_args(n, raw)[j]))

        by_core(run)

    def backward(i, n):
        p = prob[i, n]
        dp = dot(vb[n], gt[i])
        ds = (p.astype(F32) * (dp - rows[i, 0:1])).astype(BF16)
        dv_acc[n] += dot_nt(p, gft[i])
        dk_acc[n] += dot_nt(ds, qft[i])
        dqt[i] += dot(kt[n], ds)

    def send_dq(i):
        dq_tx[i] = (dqt[i] * rows[i, 1:2]).T.astype(BF16)
        put(*dq_args(i))

    def loop(lo, hi, body):
        def run(n, carry):
            body(n)
            return carry

        lax.fori_loop(lo, hi, run, 0)

    peaks = []
    for i in range(NB):
        m, mx = forward(i, mx)
        peaks.append(m)
        if i == 0:
            pending += hop(1)
        if i == 2:
            finish(0, peaks[0])
            finish(1, peaks[1])
    finish(2, peaks[2])
    finish(3, peaks[3])

    def early(i):
        def pair(n):
            backward(i, 2 * n)
            backward(i, 2 * n + 1)

        combine(i)
        loop(0, NB // 2, pair)
        send_dq(i)

    loop(0, 2, lambda t: early(1 + 2 * t))
    combine(2)
    combine(0)

    def both(t):
        n = 3 - 2 * t
        backward(2, n)
        backward(0, n)
        trade_kv(n)

    def relay_now():
        for arr in range(2):
            arrived(yr.at[arr], yr_rs.at[arr])
            relay_down(arr).start()

    passed = order(lax.rem(z - 2 * lax.rem(y + 1, 2) - c + 4, 4))

    loop(0, 2, both)
    reduce_kv(jnp.int32(3))
    backward(2, 2)
    backward(2, 0)
    send_dq(2)
    reduce_kv(jnp.int32(1))

    def final(t):
        pl.when(passed == 3 - 2 * t)(relay_now)
        n = 2 - 2 * t
        backward(0, n)
        trade_kv(n)

    loop(0, 2, final)
    reduce_kv(jnp.int32(2))
    send_dq(0)
    reduce_kv(jnp.int32(0))
    pl.when(lax.rem(passed, 2) == 0)(relay_now)

    for j in range(2):
        for n in range(2):
            arrived(dq_rx.at[j, n], dq_rs.at[j, n])
        for arr, raw in ((0, dk_rx), (1, dv_rx)):
            arrived(raw.at[:, cols(j)], kv_rs.at[arr, j])

    for copy in pending:
        copy.wait_send()
    for arr in range(2):
        for j in range(2):
            sent(*home_kv(arr, j))

    @pl.when(relay)
    def _():
        for arr in range(2):
            for n in range(NB):
                forward_kv(arr, n).wait_send()

    for i in range(NB):
        sent(*dq_args(jnp.int32(i)))
        sent(*kv_args(jnp.int32(i), dk_rx)[0])
        sib_copy(i).wait_send()
    for arr in range(2):
        relay_down(arr).wait_send()


def collect(dq_raw, dk_raw, dv_raw, dq_out, dk_out, dv_out):
    for j in range(2):
        total = dq_raw[j, 0].astype(F32) + dq_raw[j, 1].astype(F32)
        dq_out[:, j * HEAD_DIM : (j + 1) * HEAD_DIM] = total.astype(BF16)
    dk_out[...] = dk_raw[...]
    dv_out[...] = dv_raw[...]


def per_device(queries, key_states, value_states, out_grad):
    rows, width = queries.shape
    shape = jax.ShapeDtypeStruct((rows, width), BF16)
    vm = pltpu.VMEM
    dma = pltpu.SemaphoreType.DMA
    tile = (NB, BLK, HEAD_DIM)
    tile_t = (NB, HEAD_DIM, BLK)
    flops = 6 * 2 * (NB * BLK) ** 2 * HEAD_DIM
    raw = pl.pallas_call(
        kernel,
        out_shape=(jax.ShapeDtypeStruct((2, 2, BLK, HEAD_DIM), BF16), shape, shape),
        in_specs=[pl.BlockSpec(memory_space=pl.ANY)] * 4,
        out_specs=tuple([pl.BlockSpec(memory_space=pl.ANY)] * 3),
        scratch_shapes=[
            vm(tile, BF16), vm(tile, BF16), vm((2, 2, BLK, HEAD_DIM), BF16), vm((2,) + tile, BF16), vm((2, NB - 1, BLK, HEAD_DIM), BF16),
            vm(tile_t, BF16), vm((NB, AUG, BLK), BF16), vm(tile_t, BF16), vm(tile_t, BF16),
            vm(tile_t, BF16), vm(tile_t, BF16),
            vm((NB, BLK, BLK), F32), vm((NB, BLK, BLK), F32), vm((NB, NB, BLK, BLK), BF16), vm((NB, AUG, BLK), F32),
            vm((NB, 8, BLK), F32), vm((NB, 8, BLK), F32), vm((NB, 8, BLK), F32), vm(tile_t, F32),
            vm(tile, F32), vm(tile, F32),
            vm(tile, BF16), vm(tile, BF16), vm(tile, BF16), vm(tile, BF16), vm((2, BLK, HEAD_DIM), BF16),
            dma((NB,)), dma((NB,)), dma((2, 2)), dma((2, NB)), dma((2, NB - 1)), dma((NB,)), dma((NB,)), dma((2, 2)), dma((2, 2)), dma((2,)),
            dma((2, 2)), dma((2, 2)), dma((2, 2)), dma((2, NB)), dma((2, 3)), dma((NB,)), dma((NB,)), dma((NB,)), dma((NB,)), dma((2,)),
        ],
        compiler_params=pltpu.CompilerParams(
            collective_id=0, has_side_effects=True, vmem_limit_bytes=62 * 1024 * 1024
        ),
        cost_estimate=pl.CostEstimate(flops=flops, bytes_accessed=4 * rows * width * 2, transcendentals=(NB * BLK) ** 2),
    )(queries, key_states, value_states, out_grad)
    whole = pl.BlockSpec(memory_space=pltpu.VMEM)
    return pl.pallas_call(
        collect,
        out_shape=(shape, shape, shape),
        in_specs=[whole] * 3,
        out_specs=(whole,) * 3,
    )(*raw)


def solution(mesh):
    placed = (
        P("row", ("head", "col")),
        P("col", ("head", "row")),
        P("col", ("head", "row")),
        P("row", ("head", "col")),
    )
    return jax.shard_map(
        per_device,
        mesh=mesh,
        in_specs=placed,
        out_specs=(P("row", ("head", "col")), P("col", ("head", "row")), P("col", ("head", "row"))),
        check_vma=False,
    )
```
